128 devices in a mesh: dp: 4 (over x), expert: 32 (over z, y, core).
Axes of the slice: x: 4, y: 4, z: 4, core: 2. Of those that a mesh axis runs over, the one named last changes fastest.
Arguments:
- tokens: bfloat16 [16384, 2048], P(('dp', 'expert')), may hold values from -24 to 24
- expert_ids: int32 [16384, 4], P(('dp', 'expert')), may hold values from 0 to 63, all different within a row; in each aligned block of 128 rows (0 to 127, 128 to 255, ...) at most 16 rows name the same one
- gate_probs: float32 [16384, 4], P(('dp', 'expert')), may hold values from 0.05 to 1
- w_gate: bfloat16 [64, 2048, 768], P('expert'), may hold values from -0.125 to 0.125
- w_up: bfloat16 [64, 2048, 768], P('expert'), may hold values from -0.125 to 0.125
- w_down: bfloat16 [64, 768, 2048], P('expert'), may hold values from -0.21875 to 0.21875
- out_grad: bfloat16 [16384, 2048], P(('dp', 'expert')), may hold values from -24 to 24
Outputs:
- layer_out: bfloat16 [16384, 2048], P(('dp', 'expert'))
- token_grad: bfloat16 [16384, 2048], P(('dp', 'expert'))
- gate_grad: float32 [16384, 4], P(('dp', 'expert'))
- grad_gate: float32 [64, 2048, 768], P('expert', 'dp')
- grad_up: float32 [64, 2048, 768], P('expert', 'dp')
- grad_down: float32 [64, 768, 2048], P('expert', None, 'dp')
The draws below stay inside these ranges and needn't reach their ends.
Inputs may be any that keep to these rules, and one draw needn't show every extreme that they name: `expert_ids`: each token names 4 different experts. In each aligned block of 128 rows (the tokens of one device) no expert is named by more than 16 rows, a bound that some block reaches.
All inputs are finite; a program needn't handle non-finite values.
Results may differ from the reference program's by a relative error of at most 0.012.
Values may be sent and summed in bfloat16 or wider, within the bound.
A program may use at most 192 MiB of HBM per device.

```python
import math
import jax
import jax.numpy as jnp
import numpy as np
from jax import lax

D = 2048
FF = 768
TOP = 4
TOK_DEV = 128
EXPERTS = 64
TOKENS = 16384
CAP = 16
N_DP = 4
N_EXPERT = 32
DEVICES = 128


def with_spikes(drawn, own_key, source, target, parts, factor):
    def block_of(axis_at):
        return (jnp.arange(drawn.shape[axis_at]) // (drawn.shape[axis_at] // parts)).reshape((-1,) + (1,) * (drawn.ndim - 1 - axis_at))

    first = jax.random.permutation(own_key, parts)[block_of(target)]
    far = (block_of(target) + parts // 2) % parts
    return jnp.where((block_of(source) == first) | (block_of(source) == far), factor * drawn, drawn)


def levels(stream_key, dims, shards, low, high):
    def one(dim, shards_of):
        draws = jax.random.uniform(jax.random.fold_in(jax.random.fold_in(stream_key, 6), dim), (shards_of,), jnp.float32, low / len(shards), high / len(shards))
        return jnp.repeat(jnp.exp(draws), dims[dim] // shards_of).reshape((-1,) + (1,) * (len(dims) - dim - 1))

    loudness = one(*shards[0])
    for cut in shards[1:]:
        loudness = loudness * one(*cut)
    return loudness


def shared_out(key, own, number, rows, number_of, top, limit, lean):
    ranking = jax.random.permutation(key, number_of)
    packed, common = shares(number_of, rows * top, limit, lean, True), shares(number_of, rows * top, limit, lean, False)
    places = jnp.arange(number_of)

    def named(tallies, offset_by):
        used = int((tallies > 0).sum())
        fixed = max(1, used // 4)
        shifted = fixed + (places - fixed + offset_by * (used - fixed)) % max(1, number_of - fixed)
        return jnp.zeros((number_of,), jnp.int32).at[ranking[jnp.where(places < fixed, places, shifted)]].set(jnp.asarray(tallies, jnp.int32))

    tallies = jnp.where(number % 4 == 0, named(packed, number // 4), named(common, number - number // 4 - 1))
    mixed = jax.random.permutation(jax.random.fold_in(own, 3), number_of)
    giver, sink = mixed[0:number_of // 2 * 2:2], mixed[1:number_of // 2 * 2:2]
    slack = jnp.minimum(tallies[giver] - 1, limit - tallies[sink]) // 2
    slack = jnp.where((giver == ranking[0]) | (sink == ranking[0]) | (tallies[sink] == 0), 0, jnp.maximum(slack, 0))
    shifted = jax.random.randint(jax.random.fold_in(own, 4), (number_of // 2,), 0, 1 << 20) % (slack + 1)
    tallies = tallies.at[giver].add(-shifted).at[sink].add(shifted)
    items = jnp.searchsorted(jnp.cumsum(tallies), jnp.arange(rows * top), side="right").astype(jnp.int32)
    table = items.reshape(top, rows).T
    table = table[jax.random.permutation(jax.random.fold_in(own, 1), rows)]
    offset_by = jax.random.randint(jax.random.fold_in(own, 2), (rows, 1), 0, top)
    return jnp.take_along_axis(table, (jnp.arange(top)[None, :] + offset_by) % top, axis=1)


def shares(count, total, limit, lean, full):
    weights = [(1 << 20) // math.isqrt(grade ** lean) + 1 for grade in range(1, count + 1)]
    largest = limit if full else min(limit, max(-(-total // count), total * weights[0] // sum(weights)))
    least = 1 if total - largest >= count - 1 else 0
    given, surplus = [largest] + [least] * (count - 1), total - largest - least * (count - 1)
    while surplus > 0:
        free = [i for i in range(1, count) if given[i] < largest] or [i for i in range(1, count) if given[i] < limit]
        pool, remaining = sum([weights[i] for i in free]), surplus
        for i in free:
            extra = min(limit - given[i], max(1, remaining * weights[i] // pool), surplus)
            given[i] = given[i] + extra
            surplus = surplus - extra
    return np.array(given)


def scatter_about(rng, shape, width, bound, split=(), kind=jnp.bfloat16):
    gain = levels(rng, shape, split, -0.22, 0.18) if split else 1.0
    drawn = jax.random.normal(rng, shape, jnp.float32) * width * gain
    return jnp.minimum(jnp.maximum(drawn, -bound), bound).astype(kind)


def heavy_noise(rng, shape, spread, bound, shards, heavy, kind=jnp.bfloat16):
    entries = spread * jax.random.normal(rng, shape, jnp.float32)
    if shards:
        entries = entries * levels(rng, shape, shards, -0.22, 0.18)
    return jnp.clip(with_spikes(entries, jax.random.fold_in(rng, 3), *heavy), -bound, bound).astype(kind)


def setup_inputs(seed: int = 0) -> dict:
    splits = jax.random.split(jax.random.key(seed), 8)
    tokens = heavy_noise(splits[0], (TOKENS, D), 1.0, 24.0, ((0, 128),), (0, 1, 128, 5.5))
    expert_ids_keys = jax.random.split(jax.random.fold_in(splits[1], 1), TOKENS // TOK_DEV)
    expert_ids_turns = jax.random.permutation(jax.random.fold_in(splits[1], 3), TOKENS // TOK_DEV)
    expert_ids = jax.vmap(lambda own, number: shared_out(jax.random.fold_in(splits[1], 2), own, number, TOK_DEV, EXPERTS, TOP, CAP, 2))(expert_ids_keys, expert_ids_turns).reshape((TOKENS, TOP))
    gate_probs = jnp.clip(jnp.exp(math.log(1.0) - 2.9957323 * jax.random.uniform(splits[2], (TOKENS, TOP), jnp.float32) ** levels(splits[2], (TOKENS, TOP), ((0, 128),), -0.2, 0.2)), 0.05, 1.0)
    w_gate = scatter_about(splits[3], (EXPERTS, D, FF), D ** -0.5, 0.125, ((0, 32),))
    w_up = scatter_about(splits[4], (EXPERTS, D, FF), D ** -0.5, 0.125, ((0, 32),))
    w_down = scatter_about(splits[5], (EXPERTS, FF, D), FF ** -0.5, 0.21875, ((0, 32),))
    out_grad = heavy_noise(splits[6], (TOKENS, D), 1.0, 24.0, ((0, 128),), (0, 1, 128, 5.5))
    return {"tokens": tokens, "expert_ids": expert_ids, "gate_probs": gate_probs, "w_gate": w_gate, "w_up": w_up, "w_down": w_down, "out_grad": out_grad}


def silu_parts(pre_value):
    logistic = 1.0 / (1.0 + jnp.exp(-pre_value))
    return pre_value * logistic, logistic


def group_sum(left_rows, right_rows):
    left_group = left_rows.reshape(N_DP, N_EXPERT * CAP, left_rows.shape[1]).astype(jnp.float32)
    right_group = right_rows.reshape(N_DP, N_EXPERT * CAP, right_rows.shape[1]).astype(jnp.float32)
    partial_value = jnp.einsum("gsa,gsb->gab", left_group, right_group)
    partial_value = lax.optimization_barrier(partial_value.astype(jnp.bfloat16)).astype(jnp.float32)
    return jnp.sum(partial_value, axis=0)


def reference(tokens, expert_ids, gate_probs, w_gate, w_up, w_down, out_grad):
    row_count = TOKENS * TOP
    per_device = TOK_DEV * TOP
    flat_ids = expert_ids.reshape(DEVICES, per_device)

    def rank_block(id_block):
        one_hot = (id_block[:, None] == jnp.arange(EXPERTS, dtype=jnp.int32)[None, :]).astype(jnp.int32)
        return jnp.sum((jnp.cumsum(one_hot, axis=0) - 1) * one_hot, axis=1).astype(jnp.int32)

    rank_in = lax.map(rank_block, flat_ids)
    device_ids = jnp.arange(DEVICES, dtype=jnp.int32)[:, None]
    position = (device_ids * CAP + rank_in).reshape(row_count).astype(jnp.int32)
    experts_flat = expert_ids.reshape(row_count).astype(jnp.int32)
    row_table = jnp.full((EXPERTS, DEVICES * CAP), row_count, jnp.int32)
    row_table = row_table.at[experts_flat, position].set(jnp.arange(row_count, dtype=jnp.int32))

    zero_row = jnp.zeros((1, D), jnp.bfloat16)
    tokens_pad = jnp.concatenate([tokens, zero_row], axis=0)
    grad_pad = jnp.concatenate([out_grad, zero_row], axis=0)
    probs_pad = jnp.concatenate([gate_probs.reshape(row_count), jnp.zeros((1,), jnp.float32)])

    def one_expert(totals, inputs):
        mixed_acc, delta_acc, gate_acc = totals
        row_ids, gate_w, up_w, down_w = inputs
        tok_idx = jnp.where(row_ids < row_count, row_ids // TOP, TOKENS).astype(jnp.int32)
        token_rows = tokens_pad[tok_idx]
        pre_gate = jnp.dot(token_rows, gate_w, preferred_element_type=jnp.float32)
        pre_up = jnp.dot(token_rows, up_w, preferred_element_type=jnp.float32)
        activated, logistic = silu_parts(pre_gate)
        act = (activated * pre_up).astype(jnp.bfloat16)
        expert_out = jnp.dot(act, down_w, preferred_element_type=jnp.float32).astype(jnp.bfloat16)
        row_prob = probs_pad[row_ids]
        grad_rows = grad_pad[tok_idx]
        mixed_acc = mixed_acc.at[tok_idx].add(row_prob[:, None] * expert_out.astype(jnp.float32))
        gate_acc = gate_acc.at[row_ids].set(jnp.sum(grad_rows.astype(jnp.float32) * expert_out.astype(jnp.float32), axis=1))
        out_delta = (row_prob[:, None] * grad_rows.astype(jnp.float32)).astype(jnp.bfloat16)
        act_delta = jnp.dot(out_delta, down_w.T, preferred_element_type=jnp.float32)
        gate_delta = (act_delta * pre_up * logistic * (1.0 + pre_gate * (1.0 - logistic))).astype(jnp.bfloat16)
        up_delta = (act_delta * activated).astype(jnp.bfloat16)
        row_grad = (jnp.dot(gate_delta, gate_w.T, preferred_element_type=jnp.float32)
                    + jnp.dot(up_delta, up_w.T, preferred_element_type=jnp.float32)).astype(jnp.bfloat16)
        delta_acc = delta_acc.at[tok_idx].add(row_grad.astype(jnp.float32))
        sum_gate = group_sum(token_rows, gate_delta)
        sum_up = group_sum(token_rows, up_delta)
        sum_down = group_sum(act, out_delta)
        return (mixed_acc, delta_acc, gate_acc), (sum_gate, sum_up, sum_down)

    initial = (jnp.zeros((TOKENS + 1, D), jnp.float32), jnp.zeros((TOKENS + 1, D), jnp.float32),
               jnp.zeros((row_count + 1,), jnp.float32))
    finals, stacked = lax.scan(one_expert, initial, (row_table, w_gate, w_up, w_down))
    mixed_acc, delta_acc, gate_acc = finals
    grad_gate, grad_up, grad_down = stacked
    layer_out = mixed_acc[:TOKENS].astype(jnp.bfloat16)
    token_grad = delta_acc[:TOKENS].astype(jnp.bfloat16)
    gate_grad = gate_acc[:row_count].reshape(TOKENS, TOP)
    return (layer_out, token_grad, gate_grad, grad_gate, grad_up, grad_down)
```

```python
import functools

import jax
import jax.numpy as jnp
from jax import lax
from jax.experimental import pallas as pl
from jax.experimental.pallas import tpu as pltpu
from jax.sharding import PartitionSpec as P

MESH = pl.DeviceIdType.MESH
F32 = jnp.float32
BF16 = jnp.bfloat16
CAP = 16
NT = (((1,), (1,)), ((), ()))
TN = (((0,), (0,)), ((), ()))


def dot(a, b, dims=(((1,), (0,)), ((), ()))):
    return lax.dot_general(a, b, dims, preferred_element_type=F32)


def tiles(count, body):
    if count == 1:
        body(0)
    else:
        lax.fori_loop(0, count, lambda i, c: (body(i), c)[1], 0)


def span(i, size):
    return pl.ds(pl.multiple_of(i * size, size), size)


def kernel(
    n_dp, n_exp,
    route_ref, ids_ref, tok_ref, og_ref, wg_hbm, wu_hbm, wd_hbm,
    lo_ref, tg_ref, gg_ref, own_gu, own_dn, land_gu, land_dn, back,
    send, recv, tt, wg, wu, wd, act, act_t, gd, ud, pre_g, pre_u,
    part_gu, part_dn, mid_gu, mid_dn, sel, sel_t, pslot, acc,
    w_sem, disp_send, disp_recv, back_send, back_recv,
    rs_send, mid_recv, land_sem, own_sem, load_sem,
):
    dp, me = lax.axis_index("dp"), lax.axis_index("expert")
    tok, feats = tok_ref.shape
    hidden = wg.shape[1]
    rows = n_exp * CAP
    top = ids_ref.shape[1]
    right, left = lax.rem(dp + 1, n_dp), lax.rem(dp + n_dp - 1, n_dp)
    across = lax.rem(dp + 2, n_dp)
    f_tile, d_tile = min(256, hidden), min(256, feats)
    n_f, n_d = hidden // f_tile, feats // d_tile
    share = feats // n_dp

    def peer(k):
        if n_exp != 32:
            return lax.rem(me + k, n_exp)
        off = lax.rem(k * 11, 32)
        z, y, c = me // 8, lax.rem(me // 2, 4), lax.rem(me, 2)
        z = lax.rem(z + off // 8, 4)
        y = lax.rem(y + lax.rem(off // 2, 4), 4)
        c = lax.rem(c + lax.rem(off, 2), 2)
        return (z * 4 + y) * 2 + c

    barrier = pltpu.get_barrier_semaphore()

    def greet(k, carry):
        pl.semaphore_signal(barrier, inc=1, device_id={"expert": peer(k)}, device_id_type=MESH)
        return carry

    lax.fori_loop(1, n_exp, greet, 0)
    for side in (left, right):
        pl.semaphore_signal(barrier, inc=1, device_id={"dp": side}, device_id_type=MESH)

    def weights(l):
        return [
            pltpu.make_async_copy(src.at[l], dst, w_sem.at[i])
            for i, (src, dst) in enumerate(((wg_hbm, wg), (wu_hbm, wu), (wd_hbm, wd)))
        ]

    for copy in weights(0):
        copy.start()

    ids_t, probs_t = route_ref[0:top, :], route_ref[top : 2 * top, :]
    earlier = (
        lax.broadcasted_iota(jnp.int32, (tok, tok), 0)
        < lax.broadcasted_iota(jnp.int32, (tok, tok), 1)
    ).astype(F32).astype(BF16)

    def route(l):
        expert = (lax.broadcasted_iota(jnp.int32, (n_exp, tok), 0) * 2 + l).astype(F32)
        named = jnp.zeros((n_exp, tok), F32)
        prob = jnp.zeros((n_exp, tok), F32)
        for k in range(top):
            hit = expert == ids_t[k : k + 1, :]
            named = named + jnp.where(hit, 1.0, 0.0)
            prob = prob + jnp.where(hit, probs_t[k : k + 1, :], 0.0)
        rank = dot(named.astype(BF16), earlier)
        rank = jnp.where(named > 0.0, rank, -1.0)
        slot = lax.broadcasted_iota(jnp.int32, (n_exp, CAP, tok), 1).astype(F32)
        hit = jnp.where(rank[:, None, :] == slot, 1.0, 0.0)
        weight = jnp.sum(hit * prob[:, None, :], axis=2, keepdims=True)
        hit = hit.reshape(rows, tok)
        sel[l] = hit.astype(BF16)
        sel_t[l] = hit.T.astype(BF16)
        pslot[l] = weight.reshape(rows, 1)

    def fill_tokens(l):
        def body(i):
            cols = span(i, d_tile)
            send[2 * l, :, cols] = dot(sel[l], tok_ref[:, cols]).astype(BF16)
        tiles(n_d, body)

    def fill_delta(l):
        def body(i):
            cols = span(i, d_tile)
            send[2 * l + 1, :, cols] = (pslot[l] * dot(sel[l], og_ref[:, cols])).astype(BF16)
        tiles(n_d, body)

    def chunk(i):
        return pl.ds(pl.multiple_of(i * CAP, CAP), CAP)

    def exchange(i, land, send_sem, recv_sem):
        pltpu.make_async_copy(send.at[i, chunk(me)], land.at[i, chunk(me)], recv_sem.at[i]).start()

        def body(k, carry):
            to = peer(k)
            pltpu.make_async_remote_copy(
                src_ref=send.at[i, chunk(to)],
                dst_ref=land.at[i, chunk(me)],
                send_sem=send_sem.at[i],
                recv_sem=recv_sem.at[i],
                device_id={"expert": to},
                device_id_type=MESH,
            ).start()
            return carry

        lax.fori_loop(1, n_exp, body, 0)

    def wait_sent(i, sem):
        part = send.at[i, pl.ds(0, rows - CAP)]
        pltpu.make_async_copy(part, part, sem.at[i]).wait()

    def wait_landed(i, land, sem):
        pltpu.make_async_copy(land.at[i], land.at[i], sem.at[i]).wait()

    def forward(l):
        def body(i):
            cols = span(i, f_tile)
            g = dot(recv[2 * l], wg[:, cols])
            u = dot(recv[2 * l], wu[:, cols])
            pre_g[:, cols] = g
            pre_u[:, cols] = u
            a = (g * (1.0 / (1.0 + jnp.exp(-g))) * u).astype(BF16)
            act[:, cols] = a
            act_t[cols, :] = a.T
        tiles(n_f, body)

    def turn_tokens(l):
        def body(i):
            cols = span(i, d_tile)
            tt[cols, :] = recv[2 * l, :, cols].T
        tiles(n_d, body)

    def outputs(l):
        def body(i):
            cols = span(i, d_tile)
            send[2 * l, :, cols] = dot(act[...], wd[:, cols]).astype(BF16)
        tiles(n_d, body)

    def deltas(l):
        def body(i):
            cols = span(i, f_tile)
            ad = dot(recv[2 * l + 1], wd[cols, :], NT)
            g, u = pre_g[:, cols], pre_u[:, cols]
            s = 1.0 / (1.0 + jnp.exp(-g))
            gd[:, cols] = (ad * u * s * (1.0 + g * (1.0 - s))).astype(BF16)
            ud[:, cols] = (ad * (g * s)).astype(BF16)
        tiles(n_f, body)

    def input_grads(l):
        def body(i):
            cols = span(i, d_tile)
            send[2 * l + 1, :, cols] = (
                dot(gd[...], wg[cols, :], NT) + dot(ud[...], wu[cols, :], NT)
            ).astype(BF16)
        tiles(n_d, body)

    def down_part(l):
        def body(j):
            part_dn[l, j] = dot(act_t[...], recv[2 * l + 1, :, span(j, share)]).astype(BF16)
        tiles(n_dp, body)

    def gate_up_part(l, which):
        src = (gd, ud)[which]

        def body(j):
            part_gu[l, which, j] = dot(tt[span(j, share), :], src[...]).astype(BF16)
        tiles(n_dp, body)

    def views(l, which):
        if which == 2:
            return part_dn.at[l], land_dn, mid_dn, own_dn.at[l], lambda s: land_dn.at[s, l], lambda s: mid_dn.at[s, l], 1
        return (
            part_gu.at[l, which], land_gu, mid_gu, own_gu.at[l, which],
            lambda s: land_gu.at[s, l, which], lambda s: mid_gu.at[s, l, which], 0,
        )

    def reduce_begin(l, which):
        part, _, _, own, land, mid, kind = views(l, which)
        half = part.shape[1] // 2
        low, high = pl.ds(0, half), pl.ds(half, half)
        slot = 3 * l + which
        pltpu.make_async_copy(part.at[dp], own, own_sem.at[kind]).start()
        for to, side, mine, theirs in ((right, 0, low, high), (left, 1, high, low)):
            pltpu.make_async_remote_copy(
                src_ref=part.at[across, mine], dst_ref=mid(side),
                send_sem=rs_send.at[slot], recv_sem=mid_recv.at[slot],
                device_id={"dp": to}, device_id_type=MESH,
            ).start()
        for to, side, mine, theirs in ((right, 0, low, high), (left, 1, high, low)):
            pltpu.make_async_remote_copy(
                src_ref=part.at[to, theirs], dst_ref=land(side).at[theirs],
                send_sem=rs_send.at[slot], recv_sem=land_sem.at[kind],
                device_id={"dp": to}, device_id_type=MESH,
            ).start()

    def reduce_pass(l, which):
        part, _, mids, own, land, mid, kind = views(l, which)
        half = part.shape[1] // 2
        slot = 3 * l + which
        both = mid_dn.at[:, l] if which == 2 else mid_gu.at[:, l, which]
        pltpu.make_async_copy(both, both, mid_recv.at[slot]).wait()
        for to, side, start in ((right, 0, 0), (left, 1, half)):
            mine = pl.ds(start, half)
            step = half // 4

            def body(i):
                at = pl.ds(pl.multiple_of(start + i * step, step), step)
                part[to, at] = (
                    part[to, at].astype(F32) + mid(side)[span(i, step)].astype(F32)
                ).astype(BF16)

            tiles(4, body)
            pltpu.make_async_remote_copy(
                src_ref=part.at[to, mine], dst_ref=land(side).at[mine],
                send_sem=rs_send.at[slot], recv_sem=land_sem.at[kind],
                device_id={"dp": to}, device_id_type=MESH,
            ).start()

    def load_back(i):
        return pltpu.make_async_copy(back.at[i], recv.at[i], load_sem.at[i])

    def combine_out(l):
        i = 2 * l
        load_back(i).wait()
        prob = pslot[l]
        hit = sel[l].astype(F32)
        weight = (hit * prob).T
        hi = weight.astype(BF16)
        lo = (weight - hi.astype(F32)).astype(BF16)

        def body(n):
            cols = span(n, d_tile)
            value = dot(hi, recv[i, :, cols]) + dot(lo, recv[i, :, cols])
            if l == 0:
                acc[0, :, cols] = value
            else:
                lo_ref[:, cols] = (acc[0, :, cols] + value).astype(BF16)
        tiles(n_d, body)
        inner = dot(og_ref[...], recv[i], NT)
        inner = inner * sel_t[l].astype(F32)
        expert = lax.broadcasted_iota(jnp.int32, (tok, rows), 1) // CAP * 2 + l
        for k in range(top):
            hit = expert == ids_ref[:, k : k + 1]
            value = jnp.sum(jnp.where(hit, inner, 0.0), axis=1, keepdims=True)
            if l == 0:
                gg_ref[:, k : k + 1] = value
            else:
                gg_ref[:, k : k + 1] = gg_ref[:, k : k + 1] + value

    def combine_grad(l):
        i = 2 * l + 1
        load_back(i).wait()

        def body(n):
            cols = span(n, d_tile)
            value = dot(sel_t[l], recv[i, :, cols])
            if l == 0:
                acc[1, :, cols] = value
            else:
                tg_ref[:, cols] = (acc[1, :, cols] + value).astype(BF16)
        tiles(n_d, body)

    route(0)
    fill_tokens(0)
    pl.semaphore_wait(barrier, n_exp - 1 + 2)
    exchange(0, recv, disp_send, disp_recv)
    fill_delta(0)
    exchange(1, recv, disp_send, disp_recv)
    route(1)
    fill_tokens(1)
    fill_delta(1)

    for copy in weights(0):
        copy.wait()
    wait_landed(0, recv, disp_recv)
    wait_sent(0, disp_send)
    exchange(2, recv, disp_send, disp_recv)
    forward(0)
    turn_tokens(0)
    outputs(0)

    wait_landed(1, recv, disp_recv)
    wait_sent(1, disp_send)
    exchange(3, recv, disp_send, disp_recv)
    down_part(0)
    reduce_begin(0, 2)
    deltas(0)
    gate_up_part(0, 0)
    reduce_begin(0, 0)
    gate_up_part(0, 1)
    reduce_begin(0, 1)
    input_grads(0)
    for copy in weights(1):
        copy.start()

    wait_landed(2, recv, disp_recv)
    wait_sent(2, disp_send)
    for copy in weights(1):
        copy.wait()
    forward(1)
    turn_tokens(1)
    outputs(1)
    reduce_pass(0, 2)

    wait_landed(3, recv, disp_recv)
    wait_sent(3, disp_send)
    exchange(0, back, back_send, back_recv)
    exchange(1, back, back_send, back_recv)
    down_part(1)
    reduce_begin(1, 2)
    reduce_pass(0, 0)
    deltas(1)
    gate_up_part(1, 0)
    reduce_begin(1, 0)
    gate_up_part(1, 1)
    reduce_begin(1, 1)
    exchange(2, back, back_send, back_recv)
    input_grads(1)
    exchange(3, back, back_send, back_recv)
    reduce_pass(0, 1)

    for i in (0, 1):
        wait_landed(i, back, back_recv)
        load_back(i).start()
    combine_out(0)
    combine_grad(0)
    reduce_pass(1, 2)
    reduce_pass(1, 0)
    wait_landed(2, back, back_recv)
    load_back(2).start()
    combine_out(1)
    reduce_pass(1, 1)
    wait_landed(3, back, back_recv)
    load_back(3).start()
    combine_grad(1)

    for i in range(4):
        wait_sent(i, back_send)
    for which in range(3):
        for l in range(2):
            three = part_dn.at[l, pl.ds(0, 3)] if which == 2 else part_gu.at[l, which, pl.ds(0, 3)]
            pltpu.make_async_copy(three, three, rs_send.at[3 * l + which]).wait()
    pltpu.make_async_copy(own_gu, own_gu, own_sem.at[0]).wait()
    pltpu.make_async_copy(own_dn, own_dn, own_sem.at[1]).wait()
    pltpu.make_async_copy(land_gu, land_gu, land_sem.at[0]).wait()
    pltpu.make_async_copy(land_dn, land_dn, land_sem.at[1]).wait()


def shards(n_dp, n_exp, tokens, expert_ids, gate_probs, w_gate, w_up, w_down, out_grad):
    tok, feats = tokens.shape
    hidden = w_gate.shape[2]
    rows = n_exp * CAP
    share = feats // n_dp
    route = jnp.concatenate([expert_ids.astype(F32), gate_probs], axis=1).T
    vmem = pl.BlockSpec(memory_space=pltpu.VMEM)
    far = pl.BlockSpec(memory_space=pl.ANY)
    shape = jax.ShapeDtypeStruct
    top = expert_ids.shape[1]
    outs = pl.pallas_call(
        functools.partial(kernel, n_dp, n_exp),
        out_shape=[
            shape((tok, feats), BF16),
            shape((tok, feats), BF16),
            shape((tok, top), F32),
            shape((2, 2, share, hidden), BF16),
            shape((2, hidden, share), BF16),
            shape((2, 2, 2, share, hidden), BF16),
            shape((2, 2, hidden, share), BF16),
            shape((4, rows, feats), BF16),
        ],
        in_specs=[vmem] * 4 + [far] * 3,
        out_specs=[vmem] * 3 + [far] * 5,
        scratch_shapes=[
            pltpu.VMEM((4, rows, feats), BF16),
            pltpu.VMEM((4, rows, feats), BF16),
            pltpu.VMEM((feats, rows), BF16),
            pltpu.VMEM((feats, hidden), BF16),
            pltpu.VMEM((feats, hidden), BF16),
            pltpu.VMEM((hidden, feats), BF16),
            pltpu.VMEM((rows, hidden), BF16),
            pltpu.VMEM((hidden, rows), BF16),
            pltpu.VMEM((rows, hidden), BF16),
            pltpu.VMEM((rows, hidden), BF16),
            pltpu.VMEM((rows, hidden), F32),
            pltpu.VMEM((rows, hidden), F32),
            pltpu.VMEM((2, 2, n_dp, share, hidden), BF16),
            pltpu.VMEM((2, n_dp, hidden, share), BF16),
            pltpu.VMEM((2, 2, 2, share // 2, hidden), BF16),
            pltpu.VMEM((2, 2, hidden // 2, share), BF16),
            pltpu.VMEM((2, rows, tok), BF16),
            pltpu.VMEM((2, tok, rows), BF16),
            pltpu.VMEM((2, rows, 1), F32),
            pltpu.VMEM((2, tok, feats), F32),
            pltpu.SemaphoreType.DMA((3,)),
            pltpu.SemaphoreType.DMA((4,)),
            pltpu.SemaphoreType.DMA((4,)),
            pltpu.SemaphoreType.DMA((4,)),
            pltpu.SemaphoreType.DMA((4,)),
            pltpu.SemaphoreType.DMA((6,)),
            pltpu.SemaphoreType.DMA((6,)),
            pltpu.SemaphoreType.DMA((2,)),
            pltpu.SemaphoreType.DMA((2,)),
            pltpu.SemaphoreType.DMA((4,)),
        ],
        compiler_params=pltpu.CompilerParams(
            collective_id=0, has_side_effects=True, vmem_limit_bytes=62 * 2**20
        ),
        cost_estimate=pl.CostEstimate(
            flops=18 * 2 * rows * feats * hidden, bytes_accessed=60_000_000, transcendentals=4 * rows * hidden
        ),
    )(route, expert_ids, tokens, out_grad, w_gate, w_up, w_down)
    layer_out, token_grad, gate_grad, own_gu, own_dn, land_gu, land_dn, _ = outs
    wide = lambda a: a.astype(F32)
    total_gu = lambda i: wide(own_gu[:, i]) + wide(land_gu[0, :, i]) + wide(land_gu[1, :, i])
    grad_down = wide(own_dn) + wide(land_dn[0]) + wide(land_dn[1])
    return layer_out, token_grad, gate_grad, total_gu(0), total_gu(1), grad_down


def solution(mesh):
    tokens_at = P(("dp", "expert"), None)
    in_specs = (tokens_at,) * 3 + (P("expert", None, None),) * 3 + (tokens_at,)
    out_specs = (tokens_at,) * 3 + (
        P("expert", "dp", None),
        P("expert", "dp", None),
        P("expert", None, "dp"),
    )
    body = functools.partial(shards, mesh.shape["dp"], mesh.shape["expert"])
    return jax.shard_map(body, mesh=mesh, in_specs=in_specs, out_specs=out_specs, check_vma=False)
```

```python
import functools

import jax
import jax.numpy as jnp
from jax import lax
from jax.experimental import pallas as pl
from jax.experimental.pallas import tpu as pltpu
from jax.sharding import PartitionSpec as P

MESH = pl.DeviceIdType.MESH
F32 = jnp.float32
BF16 = jnp.bfloat16
CAP = 16
NT = (((1,), (1,)), ((), ()))
TN = (((0,), (0,)), ((), ()))


def dot(a, b, dims=(((1,), (0,)), ((), ()))):
    return lax.dot_general(a, b, dims, preferred_element_type=F32)


def tiles(count, body):
    if count == 1:
        body(0)
    else:
        lax.fori_loop(0, count, lambda i, c: (body(i), c)[1], 0)


def span(i, size):
    return pl.ds(pl.multiple_of(i * size, size), size)


def kernel(
    n_dp, n_exp,
    ids_ref, probs_ref, tok_ref, og_ref, wg_hbm, wu_hbm, wd_hbm,
    lo_ref, tg_ref, gg_ref, sum_gu, sum_dn, land_gu, land_dn, back,
    send, recv, tt, wg, wu, wd, act, act_t, gd, ud, pre_g, pre_u,
    part_gu, part_dn, mid_gu, mid_dn, sel, sel_t, pslot, acc,
    w_sem, disp_send, tok_recv, delta_recv, back_send, back_recv,
    rs_send, mid_recv, land_recv, sum_sem, load_sem,
):
    dp, me = lax.axis_index("dp"), lax.axis_index("expert")
    tok, feats = tok_ref.shape
    hidden = wg.shape[1]
    rows = n_exp * CAP
    top = ids_ref.shape[0]
    right, left = lax.rem(dp + 1, n_dp), lax.rem(dp + n_dp - 1, n_dp)
    across = lax.rem(dp + 2, n_dp)
    f_tile, d_tile = min(256, hidden), min(256, feats)
    n_f, n_d = hidden // f_tile, feats // d_tile
    share = feats // n_dp

    def peer(k):
        if n_exp != 32:
            return lax.rem(me + k, n_exp)
        off = lax.rem(k * 11, 32)
        z, y, c = me // 8, lax.rem(me // 2, 4), lax.rem(me, 2)
        z = lax.rem(z + off // 8, 4)
        y = lax.rem(y + lax.rem(off // 2, 4), 4)
        c = lax.rem(c + lax.rem(off, 2), 2)
        return (z * 4 + y) * 2 + c

    barrier = pltpu.get_barrier_semaphore()

    def greet(k, carry):
        pl.semaphore_signal(barrier, inc=1, device_id={"expert": peer(k)}, device_id_type=MESH)
        return carry

    lax.fori_loop(1, n_exp, greet, 0)
    for side in (left, right):
        pl.semaphore_signal(barrier, inc=1, device_id={"dp": side}, device_id_type=MESH)

    def weights(l):
        return [
            pltpu.make_async_copy(src.at[l], dst, w_sem.at[i])
            for i, (src, dst) in enumerate(((wg_hbm, wg), (wu_hbm, wu), (wd_hbm, wd)))
        ]

    for copy in weights(0):
        copy.start()

    ids_t, probs_t = ids_ref[...], probs_ref[...]
    earlier = (
        lax.broadcasted_iota(jnp.int32, (tok, tok), 0)
        < lax.broadcasted_iota(jnp.int32, (tok, tok), 1)
    ).astype(F32).astype(BF16)

    def route(l):
        expert = lax.broadcasted_iota(jnp.int32, (n_exp, tok), 0) * 2 + l
        named = jnp.zeros((n_exp, tok), F32)
        prob = jnp.zeros((n_exp, tok), F32)
        for k in range(top):
            hit = expert == ids_t[k : k + 1, :]
            named = named + jnp.where(hit, 1.0, 0.0)
            prob = prob + jnp.where(hit, probs_t[k : k + 1, :], 0.0)
        rank = dot(named.astype(BF16), earlier)
        rank = jnp.where(named > 0.0, rank, -1.0)
        slot = lax.broadcasted_iota(jnp.int32, (n_exp, CAP, tok), 1).astype(F32)
        hit = jnp.where(rank[:, None, :] == slot, 1.0, 0.0)
        weight = jnp.sum(hit * prob[:, None, :], axis=2, keepdims=True)
        hit = hit.reshape(rows, tok)
        sel[l] = hit.astype(BF16)
        sel_t[l] = hit.T.astype(BF16)
        pslot[l] = weight.reshape(rows, 1)

    def fill_tokens(l):
        def body(i):
            cols = span(i, d_tile)
            send[2 * l, :, cols] = dot(sel[l], tok_ref[:, cols]).astype(BF16)
        tiles(n_d, body)

    def fill_delta(l):
        def body(i):
            cols = span(i, d_tile)
            send[2 * l + 1, :, cols] = (pslot[l] * dot(sel[l], og_ref[:, cols])).astype(BF16)
        tiles(n_d, body)

    def chunk(i):
        return pl.ds(pl.multiple_of(i * CAP, CAP), CAP)

    everything = pl.ds(0, feats)

    def exchange(i, land, cols, send_sem, recv_sem):
        pltpu.make_async_copy(
            send.at[i, chunk(me), cols], land.at[i, chunk(me), cols], recv_sem
        ).start()

        def body(k, carry):
            to = peer(k)
            pltpu.make_async_remote_copy(
                src_ref=send.at[i, chunk(to), cols],
                dst_ref=land.at[i, chunk(me), cols],
                send_sem=send_sem,
                recv_sem=recv_sem,
                device_id={"expert": to},
                device_id_type=MESH,
            ).start()
            return carry

        lax.fori_loop(1, n_exp, body, 0)

    def wait_sent(i, sem):
        part = send.at[i, pl.ds(0, rows - CAP)]
        pltpu.make_async_copy(part, part, sem.at[i]).wait()

    def wait_landed(view, sem):
        pltpu.make_async_copy(view, view, sem).wait()

    order = (across, right, left, dp)

    def send_tokens(l):
        exchange(2 * l, recv, everything, disp_send.at[2 * l], tok_recv.at[l])

    def send_delta(l):
        for n, j in enumerate(order):
            exchange(2 * l + 1, recv, span(j, share), disp_send.at[2 * l + 1], delta_recv.at[l, n])

    def tokens_landed(l):
        wait_landed(recv.at[2 * l], tok_recv.at[l])

    def delta_landed(l, n):
        wait_landed(recv.at[2 * l + 1, :, span(order[n], share)], delta_recv.at[l, n])

    def send_back(i):
        exchange(i, back, everything, back_send.at[i], back_recv.at[i])

    def forward(l):
        def body(i):
            cols = span(i, f_tile)
            g = dot(recv[2 * l], wg[:, cols])
            u = dot(recv[2 * l], wu[:, cols])
            pre_g[:, cols] = g
            pre_u[:, cols] = u
            a = (g * (1.0 / (1.0 + jnp.exp(-g))) * u).astype(BF16)
            act[:, cols] = a
            act_t[cols, :] = a.T
        tiles(n_f, body)

    def turn_tokens(l):
        def body(i):
            cols = span(i, d_tile)
            tt[cols, :] = recv[2 * l, :, cols].T
        tiles(n_d, body)

    def outputs(l):
        def body(i):
            cols = span(i, d_tile)
            send[2 * l, :, cols] = dot(act[...], wd[:, cols]).astype(BF16)
        tiles(n_d, body)

    def deltas(l):
        def body(i):
            cols = span(i, f_tile)
            ad = dot(recv[2 * l + 1], wd[cols, :], NT)
            g, u = pre_g[:, cols], pre_u[:, cols]
            s = 1.0 / (1.0 + jnp.exp(-g))
            gd[:, cols] = (ad * u * s * (1.0 + g * (1.0 - s))).astype(BF16)
            ud[:, cols] = (ad * (g * s)).astype(BF16)
        tiles(n_f, body)

    def input_grads(l):
        def body(i):
            cols = span(i, d_tile)
            send[2 * l + 1, :, cols] = (
                dot(gd[...], wg[cols, :], NT) + dot(ud[...], wu[cols, :], NT)
            ).astype(BF16)
        tiles(n_d, body)

    def views(l, which):
        if which == 2:
            return part_dn.at[l], lambda s: land_dn.at[s, l], lambda s: mid_dn.at[s, l]
        return part_gu.at[l, which], lambda s: land_gu.at[s, l, which], lambda s: mid_gu.at[s, l, which]

    def post(l, which, src, dst, sem, to):
        pltpu.make_async_remote_copy(
            src_ref=src, dst_ref=dst, send_sem=rs_send.at[3 * l + which], recv_sem=sem.at[3 * l + which],
            device_id={"dp": to}, device_id_type=MESH,
        ).start()

    def reduce_begin(l, which, make, ready=None):
        part, land, mid = views(l, which)
        half = part.shape[1] // 2
        low, high = pl.ds(0, half), pl.ds(half, half)
        for n, j in enumerate(order):
            if ready is not None:
                ready(n)
            make(j)
            if n == 0:
                post(l, which, part.at[j, low], mid(0), mid_recv, right)
                post(l, which, part.at[j, high], mid(1), mid_recv, left)
            elif n == 1:
                post(l, which, part.at[j, high], land(0).at[high], land_recv, right)
            elif n == 2:
                post(l, which, part.at[j, low], land(1).at[low], land_recv, left)

    def down_part(l):
        def make(j):
            def body(i):
                at = span(i, f_tile)
                part_dn[l, j, at] = dot(act_t[at, :], recv[2 * l + 1, :, span(j, share)]).astype(BF16)

            tiles(n_f, body)

        reduce_begin(l, 2, make, lambda n: delta_landed(l, n))

    def gate_up_part(l, which):
        src = (gd, ud)[which]

        def make(j):
            def body(i):
                at = span(i, d_tile)
                turned = tt[pl.ds(pl.multiple_of(j * share + i * d_tile, d_tile), d_tile), :]
                part_gu[l, which, j, at] = dot(turned, src[...]).astype(BF16)

            tiles(share // d_tile, body)

        reduce_begin(l, which, make)

    def reduce_pass(l, which):
        part, land, mid = views(l, which)
        half = part.shape[1] // 2
        both = mid_dn.at[:, l] if which == 2 else mid_gu.at[:, l, which]
        wait_landed(both, mid_recv.at[3 * l + which])
        for to, side, start in ((right, 0, 0), (left, 1, half)):
            step = half // 4

            def body(i):
                at = pl.ds(pl.multiple_of(start + i * step, step), step)
                part[to, at] = (
                    part[to, at].astype(F32) + mid(side)[span(i, step)].astype(F32)
                ).astype(BF16)

            tiles(4, body)
            mine = pl.ds(start, half)
            post(l, which, part.at[to, mine], land(side).at[mine], land_recv, to)

    def landing(l, which, side):
        if which == 2:
            return land_dn.at[side, l], wd.at[:, pl.ds((2 * l + side) * share, share)]
        return land_gu.at[side, l, which], (wg, wu)[which].at[pl.ds((2 * l + side) * share, share)]

    def fetch(l, which):
        return [
            pltpu.make_async_copy(*landing(l, which, side), sum_sem.at[3 * l + which, side])
            for side in range(2)
        ]

    def reduce_fetch(l, which):
        both = land_dn.at[:, l] if which == 2 else land_gu.at[:, l, which]
        wait_landed(both, land_recv.at[3 * l + which])
        for copy in fetch(l, which):
            copy.start()

    def total_out(l, which):
        src, dst = (part_dn.at[l], sum_dn.at[l]) if which == 2 else (part_gu.at[l, which], sum_gu.at[which, l])
        return pltpu.make_async_copy(src.at[dp], dst, sum_sem.at[3 * l + which, 2])

    def reduce_end(l, which):
        for copy in fetch(l, which):
            copy.wait()
        part = views(l, which)[0]
        first, second = (landing(l, which, side)[1] for side in range(2))
        step = part.shape[1] // 4

        def body(i):
            at = span(i, step)
            part[dp, at] = (
                part[dp, at].astype(F32) + first[at].astype(F32) + second[at].astype(F32)
            ).astype(BF16)

        tiles(4, body)
        total_out(l, which).start()

    def load_back(i):
        return pltpu.make_async_copy(back.at[i], recv.at[i], load_sem.at[i])

    def combine_out(l):
        i = 2 * l
        load_back(i).wait()
        prob = pslot[l]
        hit = sel[l].astype(F32)
        weight = (hit * prob).T
        hi = weight.astype(BF16)
        lo = (weight - hi.astype(F32)).astype(BF16)

        def body(n):
            cols = span(n, d_tile)
            value = dot(hi, recv[i, :, cols]) + dot(lo, recv[i, :, cols])
            if l == 0:
                acc[0, :, cols] = value
            else:
                lo_ref[:, cols] = (acc[0, :, cols] + value).astype(BF16)
        tiles(n_d, body)
        inner = dot(recv[i], og_ref[...], NT) * hit
        inner = jnp.sum(inner.reshape(n_exp, CAP, tok), axis=1)
        expert = lax.broadcasted_iota(jnp.int32, (n_exp, tok), 0) * 2 + l
        for k in range(top):
            mine = jnp.where(expert == ids_t[k : k + 1, :], inner, 0.0)
            value = jnp.sum(mine, axis=0, keepdims=True)
            if l == 0:
                gg_ref[k : k + 1, :] = value
            else:
                gg_ref[k : k + 1, :] = gg_ref[k : k + 1, :] + value

    def combine_grad(l):
        i = 2 * l + 1
        load_back(i).wait()

        def body(n):
            cols = span(n, d_tile)
            value = dot(sel_t[l], recv[i, :, cols])
            if l == 0:
                acc[1, :, cols] = value
            else:
                tg_ref[:, cols] = (acc[1, :, cols] + value).astype(BF16)
        tiles(n_d, body)

    route(0)
    fill_tokens(0)
    pl.semaphore_wait(barrier, n_exp - 1 + 2)
    send_tokens(0)
    fill_delta(0)
    send_delta(0)
    route(1)
    fill_tokens(1)
    send_tokens(1)
    fill_delta(1)
    send_delta(1)

    for copy in weights(0):
        copy.wait()
    tokens_landed(0)
    forward(0)
    down_part(0)
    turn_tokens(0)
    reduce_pass(0, 2)
    deltas(0)
    gate_up_part(0, 0)
    gate_up_part(0, 1)
    wait_sent(0, disp_send)
    outputs(0)
    send_back(0)
    wait_sent(1, disp_send)
    input_grads(0)
    send_back(1)
    for copy in weights(1):
        copy.start()

    tokens_landed(1)
    for copy in weights(1):
        copy.wait()
    forward(1)
    turn_tokens(1)
    reduce_pass(0, 0)
    wait_sent(2, disp_send)
    outputs(1)
    send_back(2)
    reduce_pass(0, 1)
    down_part(1)
    deltas(1)
    gate_up_part(1, 0)
    gate_up_part(1, 1)
    wait_sent(3, disp_send)
    input_grads(1)
    send_back(3)

    reduce_fetch(0, 2)
    reduce_end(0, 2)
    reduce_fetch(0, 0)
    reduce_fetch(0, 1)
    wait_landed(back.at[0], back_recv.at[0])
    load_back(0).start()
    reduce_end(0, 0)
    reduce_end(0, 1)
    combine_out(0)
    reduce_pass(1, 2)
    wait_landed(back.at[1], back_recv.at[1])
    load_back(1).start()
    combine_grad(0)
    reduce_pass(1, 0)
    reduce_pass(1, 1)
    wait_landed(back.at[2], back_recv.at[2])
    load_back(2).start()
    combine_out(1)
    for which in (2, 0):
        reduce_fetch(1, which)
        reduce_end(1, which)
    wait_landed(back.at[3], back_recv.at[3])
    load_back(3).start()
    reduce_fetch(1, 1)
    combine_grad(1)
    reduce_end(1, 1)

    for i in range(4):
        wait_sent(i, back_send)
    for l in range(2):
        for which in range(3):
            three = part_dn.at[l, pl.ds(0, 3)] if which == 2 else part_gu.at[l, which, pl.ds(0, 3)]
            wait_landed(three, rs_send.at[3 * l + which])
            total_out(l, which).wait()


def shards(n_dp, n_exp, tokens, expert_ids, gate_probs, w_gate, w_up, w_down, out_grad):
    tok, feats = tokens.shape
    hidden = w_gate.shape[2]
    rows = n_exp * CAP
    share = feats // n_dp
    vmem = pl.BlockSpec(memory_space=pltpu.VMEM)
    far = pl.BlockSpec(memory_space=pl.ANY)
    shape = jax.ShapeDtypeStruct
    top = expert_ids.shape[1]
    outs = pl.pallas_call(
        functools.partial(kernel, n_dp, n_exp),
        out_shape=[
            shape((tok, feats), BF16),
            shape((tok, feats), BF16),
            shape((top, tok), F32),
            shape((2, 2, share, hidden), BF16),
            shape((2, hidden, share), BF16),
            shape((2, 2, 2, share, hidden), BF16),
            shape((2, 2, hidden, share), BF16),
            shape((4, rows, feats), BF16),
        ],
        in_specs=[vmem] * 4 + [far] * 3,
        out_specs=[vmem] * 3 + [far] * 5,
        scratch_shapes=[
            pltpu.VMEM((4, rows, feats), BF16),
            pltpu.VMEM((4, rows, feats), BF16),
            pltpu.VMEM((feats, rows), BF16),
            pltpu.VMEM((feats, hidden), BF16),
            pltpu.VMEM((feats, hidden), BF16),
            pltpu.VMEM((hidden, feats), BF16),
            pltpu.VMEM((rows, hidden), BF16),
            pltpu.VMEM((hidden, rows), BF16),
            pltpu.VMEM((rows, hidden), BF16),
            pltpu.VMEM((rows, hidden), BF16),
            pltpu.VMEM((rows, hidden), F32),
            pltpu.VMEM((rows, hidden), F32),
            pltpu.VMEM((2, 2, n_dp, share, hidden), BF16),
            pltpu.VMEM((2, n_dp, hidden, share), BF16),
            pltpu.VMEM((2, 2, 2, share // 2, hidden), BF16),
            pltpu.VMEM((2, 2, hidden // 2, share), BF16),
            pltpu.VMEM((2, rows, tok), BF16),
            pltpu.VMEM((2, tok, rows), BF16),
            pltpu.VMEM((2, rows, 1), F32),
            pltpu.VMEM((2, tok, feats), F32),
            pltpu.SemaphoreType.DMA((3,)),
            pltpu.SemaphoreType.DMA((4,)),
            pltpu.SemaphoreType.DMA((2,)),
            pltpu.SemaphoreType.DMA((2, 4)),
            pltpu.SemaphoreType.DMA((4,)),
            pltpu.SemaphoreType.DMA((4,)),
            pltpu.SemaphoreType.DMA((6,)),
            pltpu.SemaphoreType.DMA((6,)),
            pltpu.SemaphoreType.DMA((6,)),
            pltpu.SemaphoreType.DMA((6, 3)),
            pltpu.SemaphoreType.DMA((4,)),
        ],
        compiler_params=pltpu.CompilerParams(
            collective_id=0, has_side_effects=True, vmem_limit_bytes=62 * 2**20
        ),
        cost_estimate=pl.CostEstimate(
            flops=18 * 2 * rows * feats * hidden, bytes_accessed=60_000_000, transcendentals=4 * rows * hidden
        ),
    )(expert_ids.T, gate_probs.T, tokens, out_grad, w_gate, w_up, w_down)
    layer_out, token_grad, gate_grad, sum_gu, sum_dn, *_ = outs
    return layer_out, token_grad, gate_grad.T, sum_gu[0].astype(F32), sum_gu[1].astype(F32), sum_dn.astype(F32)


def solution(mesh):
    tokens_at = P(("dp", "expert"), None)
    in_specs = (tokens_at,) * 3 + (P("expert", None, None),) * 3 + (tokens_at,)
    out_specs = (tokens_at,) * 3 + (
        P("expert", "dp", None),
        P("expert", "dp", None),
        P("expert", None, "dp"),
    )
    body = functools.partial(shards, mesh.shape["dp"], mesh.shape["expert"])
    return jax.shard_map(body, mesh=mesh, in_specs=in_specs, out_specs=out_specs, check_vma=False)
```

```python
import functools

import jax
import jax.numpy as jnp
from jax import lax
from jax.experimental import pallas as pl
from jax.experimental.pallas import tpu as pltpu
from jax.sharding import PartitionSpec as P

MESH = pl.DeviceIdType.MESH
F32 = jnp.float32
BF16 = jnp.bfloat16
CAP = 16
NT = (((1,), (1,)), ((), ()))
TN = (((0,), (0,)), ((), ()))


def dot(a, b, dims=(((1,), (0,)), ((), ()))):
    return lax.dot_general(a, b, dims, preferred_element_type=F32)


def tiles(count, body):
    if count == 1:
        body(0)
    else:
        lax.fori_loop(0, count, lambda i, c: (body(i), c)[1], 0)


def span(i, size):
    return pl.ds(pl.multiple_of(i * size, size), size)


def kernel(
    n_dp, n_exp,
    ids_ref, probs_ref, tok_ref, og_ref, wg_hbm, wu_hbm, wd_hbm,
    lo_ref, tg_ref, gg_ref, sum_gu, sum_dn, land_gu, land_dn, back,
    send, recv, tt, wg, wu, wd, act, act_t, gd, ud, pre_g, pre_u,
    part_gu, part_dn, mid_gu, mid_dn, sel, pslot, acc,
    w_sem, disp_send, tok_recv, delta_recv, back_send, back_recv, last_recv,
    rs_send, mid_recv, land_recv, sum_sem, load_sem,
):
    dp, me = lax.axis_index("dp"), lax.axis_index("expert")
    tok, feats = tok_ref.shape
    hidden = wg.shape[1]
    rows = n_exp * CAP
    top = ids_ref.shape[0]
    right, left = lax.rem(dp + 1, n_dp), lax.rem(dp + n_dp - 1, n_dp)
    across = lax.rem(dp + 2, n_dp)
    f_tile, d_tile = min(256, hidden), min(256, feats)
    n_f, n_d = hidden // f_tile, feats // d_tile
    share = feats // n_dp

    def peer(k):
        if n_exp != 32:
            return lax.rem(me + k, n_exp)
        off = lax.rem(k * 11, 32)
        z, y, c = me // 8, lax.rem(me // 2, 4), lax.rem(me, 2)
        z = lax.rem(z + off // 8, 4)
        y = lax.rem(y + lax.rem(off // 2, 4), 4)
        c = lax.rem(c + lax.rem(off, 2), 2)
        return (z * 4 + y) * 2 + c

    barrier = pltpu.get_barrier_semaphore()

    def greet(k, carry):
        pl.semaphore_signal(barrier, inc=1, device_id={"expert": peer(k)}, device_id_type=MESH)
        return carry

    lax.fori_loop(1, n_exp, greet, 0)
    for side in (left, right):
        pl.semaphore_signal(barrier, inc=1, device_id={"dp": side}, device_id_type=MESH)

    def weights(l):
        return [
            pltpu.make_async_copy(src.at[l], dst, w_sem.at[i])
            for i, (src, dst) in enumerate(((wg_hbm, wg), (wu_hbm, wu), (wd_hbm, wd)))
        ]

    for copy in weights(0):
        copy.start()

    ids_t, probs_t = ids_ref[...], probs_ref[...]
    earlier = (
        lax.broadcasted_iota(jnp.int32, (tok, tok), 0)
        < lax.broadcasted_iota(jnp.int32, (tok, tok), 1)
    ).astype(F32).astype(BF16)

    def route(l):
        expert = lax.broadcasted_iota(jnp.int32, (n_exp, tok), 0) * 2 + l
        named = jnp.zeros((n_exp, tok), F32)
        prob = jnp.zeros((n_exp, tok), F32)
        for k in range(top):
            hit = expert == ids_t[k : k + 1, :]
            named = named + jnp.where(hit, 1.0, 0.0)
            prob = prob + jnp.where(hit, probs_t[k : k + 1, :], 0.0)
        rank = dot(named.astype(BF16), earlier)
        rank = jnp.where(named > 0.0, rank, -1.0)
        slot = lax.broadcasted_iota(jnp.int32, (n_exp, CAP, tok), 1).astype(F32)
        hit = jnp.where(rank[:, None, :] == slot, 1.0, 0.0)
        weight = jnp.sum(hit * prob[:, None, :], axis=2, keepdims=True)
        hit = hit.reshape(rows, tok)
        sel[l] = hit.astype(BF16)
        pslot[l] = weight.reshape(rows, 1)

    def fill_tokens(l, h):
        def body(i):
            cols = span(i + h * (n_d // 2), d_tile)
            send[2 * l, :, cols] = dot(sel[l], tok_ref[:, cols]).astype(BF16)
        tiles(n_d // 2, body)

    def fill_delta(l):
        def body(i):
            cols = span(i, d_tile)
            send[2 * l + 1, :, cols] = (pslot[l] * dot(sel[l], og_ref[:, cols])).astype(BF16)
        tiles(n_d, body)

    def chunk(i):
        return pl.ds(pl.multiple_of(i * CAP, CAP), CAP)

    everything = pl.ds(0, feats)

    def exchange(i, land, cols, send_sem, recv_sem):
        pltpu.make_async_copy(
            send.at[i, chunk(me), cols], land.at[i, chunk(me), cols], recv_sem
        ).start()

        def body(k, carry):
            to = peer(k)
            pltpu.make_async_remote_copy(
                src_ref=send.at[i, chunk(to), cols],
                dst_ref=land.at[i, chunk(me), cols],
                send_sem=send_sem,
                recv_sem=recv_sem,
                device_id={"expert": to},
                device_id_type=MESH,
            ).start()
            return carry

        lax.fori_loop(1, n_exp, body, 0)

    def wait_sent(i, sem):
        part = send.at[i, pl.ds(0, rows - CAP)]
        pltpu.make_async_copy(part, part, sem.at[i]).wait()

    def wait_landed(view, sem):
        pltpu.make_async_copy(view, view, sem).wait()

    half_share = share // 2
    pieces = tuple(
        (j, h * half_share, half_share)
        for j, h in ((across, 0), (across, 1), (right, 1), (left, 0), (right, 0), (left, 1))
    ) + ((dp, 0, share),)
    own = len(pieces) - 1

    def piece(n):
        j, start, size = pieces[n]
        return pl.ds(pl.multiple_of(j * share + start, half_share), size)

    def send_tokens(l, cols):
        exchange(2 * l, recv, cols, disp_send.at[2 * l], tok_recv.at[l])

    def send_delta(l):
        for n in range(len(pieces)):
            exchange(2 * l + 1, recv, piece(n), disp_send.at[2 * l + 1], delta_recv.at[l, n])

    def tokens_landed(l):
        wait_landed(recv.at[2 * l], tok_recv.at[l])

    def delta_landed(l, n):
        wait_landed(recv.at[2 * l + 1, :, piece(n)], delta_recv.at[l, n])

    def send_back(i):
        exchange(i, back, everything, back_send.at[i], back_recv.at[i])

    def forward(l):
        def body(i):
            cols = span(i, f_tile)
            g = dot(recv[2 * l], wg[:, cols])
            u = dot(recv[2 * l], wu[:, cols])
            pre_g[:, cols] = g
            pre_u[:, cols] = u
            a = (g * (1.0 / (1.0 + jnp.exp(-g))) * u).astype(BF16)
            act[:, cols] = a
            act_t[cols, :] = a.T
        tiles(n_f, body)

    def turn_tokens(l):
        def body(i):
            cols = span(i, d_tile)
            tt[cols, :] = recv[2 * l, :, cols].T
        tiles(n_d, body)

    def outputs(l):
        def body(i):
            cols = span(i, d_tile)
            send[2 * l, :, cols] = dot(act[...], wd[:, cols]).astype(BF16)
        tiles(n_d, body)

    def deltas(l):
        def body(i):
            cols = span(i, f_tile)
            ad = dot(recv[2 * l + 1], wd[cols, :], NT)
            g, u = pre_g[:, cols], pre_u[:, cols]
            s = 1.0 / (1.0 + jnp.exp(-g))
            gd[:, cols] = (ad * u * s * (1.0 + g * (1.0 - s))).astype(BF16)
            ud[:, cols] = (ad * (g * s)).astype(BF16)
        tiles(n_f, body)

    def input_grads(l):
        def body(i):
            cols = span(i, d_tile)
            send[2 * l + 1, :, cols] = (
                dot(gd[...], wg[cols, :], NT) + dot(ud[...], wu[cols, :], NT)
            ).astype(BF16)
        tiles(n_d, body)

    def views(l, which):
        if which == 2:
            return part_dn.at[l], lambda s: land_dn.at[s, l], lambda s: mid_dn.at[s, l]
        return part_gu.at[l, which], lambda s: land_gu.at[s, l, which], lambda s: mid_gu.at[s, l, which]

    def post(l, which, src, dst, sem, to):
        pltpu.make_async_remote_copy(
            src_ref=src, dst_ref=dst, send_sem=rs_send.at[3 * l + which], recv_sem=sem.at[3 * l + which],
            device_id={"dp": to}, device_id_type=MESH,
        ).start()

    def half(ref, which, h):
        at = pl.ds(h * half_share, half_share)
        return ref.at[:, at] if which == 2 else ref.at[at]

    def post_across(l, which, h):
        part, _, mid = views(l, which)
        post(l, which, half(part.at[across], which, h), mid(h), mid_recv, (right, left)[h])

    def post_direct(l, which, side):
        part, land, _ = views(l, which)
        to = (right, left)[side]
        post(l, which, half(part.at[to], which, 1 - side), half(land(side), which, 1 - side), land_recv, to)

    def make_down(l, n):
        j, start, size = pieces[n]

        def body(i):
            at = span(i, f_tile)
            part_dn[l, j, at, pl.ds(start, size)] = dot(act_t[at, :], recv[2 * l + 1, :, piece(n)]).astype(BF16)

        tiles(n_f, body)

    def down_part(l, meanwhile, later):
        for h in range(2):
            delta_landed(l, h)
            make_down(l, h)
            post_across(l, 2, h)
        for side in range(2):
            delta_landed(l, 2 + side)
            make_down(l, 2 + side)
            post_direct(l, 2, side)
        meanwhile()
        for n in (4, 5):
            delta_landed(l, n)
            make_down(l, n)
        later()
        delta_landed(l, own)

    def gate_up_part(l, which):
        src = (gd, ud)[which]
        for n, j in enumerate((across, right, left, dp)):

            def body(i):
                at = span(i, d_tile)
                turned = tt[pl.ds(pl.multiple_of(j * share + i * d_tile, d_tile), d_tile), :]
                part_gu[l, which, j, at] = dot(turned, src[...]).astype(BF16)

            tiles(share // d_tile, body)
            if n == 0:
                post_across(l, which, 0)
                post_across(l, which, 1)
            elif n < 3:
                post_direct(l, which, n - 1)

    def reduce_pass(l, which):
        part, land, mid = views(l, which)
        both = mid_dn.at[:, l] if which == 2 else mid_gu.at[:, l, which]
        wait_landed(both, mid_recv.at[3 * l + which])
        for side, to in enumerate((right, left)):
            mine, passed = half(part.at[to], which, side), mid(side)

            def body(i):
                at = span(i, mine.shape[0] // 4)
                mine[at, :] = (mine[at, :].astype(F32) + passed[at, :].astype(F32)).astype(BF16)

            tiles(4, body)
            post(l, which, mine, half(land(side), which, side), land_recv, to)

    def landing(l, which, side):
        if which == 2:
            return land_dn.at[side, l], wd.at[:, pl.ds((2 * l + side) * share, share)]
        return land_gu.at[side, l, which], (wg, wu)[which].at[pl.ds((2 * l + side) * share, share)]

    def fetch(l, which):
        return [
            pltpu.make_async_copy(*landing(l, which, side), sum_sem.at[3 * l + which, side])
            for side in range(2)
        ]

    def reduce_fetch(l, which):
        both = land_dn.at[:, l] if which == 2 else land_gu.at[:, l, which]
        wait_landed(both, land_recv.at[3 * l + which])
        for copy in fetch(l, which):
            copy.start()

    def total_out(l, which):
        src, dst = (part_dn.at[l], sum_dn.at[l]) if which == 2 else (part_gu.at[l, which], sum_gu.at[which, l])
        return pltpu.make_async_copy(src.at[dp], dst, sum_sem.at[3 * l + which, 2])

    def reduce_end(l, which):
        for copy in fetch(l, which):
            copy.wait()
        part = views(l, which)[0]
        first, second = (landing(l, which, side)[1] for side in range(2))
        step = part.shape[1] // 4

        def body(i):
            at = span(i, step)
            part[dp, at] = (
                part[dp, at].astype(F32) + first[at].astype(F32) + second[at].astype(F32)
            ).astype(BF16)

        tiles(4, body)
        total_out(l, which).start()

    def load_back(i, cols, n=0):
        return pltpu.make_async_copy(back.at[i, :, cols], recv.at[i, :, cols], load_sem.at[i + n])

    def back_landed(i):
        wait_landed(back.at[i], back_recv.at[i])
        load_back(i, everything).start()

    def combine_out(l):
        i = 2 * l
        hit = sel[l].astype(F32)
        weight = (hit * pslot[l]).T
        hi = weight.astype(BF16)
        lo = (weight - hi.astype(F32)).astype(BF16)
        back_landed(i)
        load_back(i, everything).wait()

        def body(n):
            cols = span(n, d_tile)
            value = dot(hi, recv[i, :, cols]) + dot(lo, recv[i, :, cols])
            if l == 0:
                acc[0, :, cols] = value
            else:
                lo_ref[:, cols] = (acc[0, :, cols] + value).astype(BF16)
        tiles(n_d, body)
        inner = dot(recv[i], og_ref[...], NT) * hit
        inner = jnp.sum(inner.reshape(n_exp, CAP, tok), axis=1)
        expert = lax.broadcasted_iota(jnp.int32, (n_exp, tok), 0) * 2 + l
        for k in range(top):
            mine = jnp.where(expert == ids_t[k : k + 1, :], inner, 0.0)
            value = jnp.sum(mine, axis=0, keepdims=True)
            if l == 0:
                gg_ref[k : k + 1, :] = value
            else:
                gg_ref[k : k + 1, :] = gg_ref[k : k + 1, :] + value

    def combine_grad_first():
        hit = sel[0].astype(F32).T.astype(BF16)
        back_landed(1)
        load_back(1, everything).wait()

        def body(n):
            cols = span(n, d_tile)
            acc[1, :, cols] = dot(hit, recv[1, :, cols])
        tiles(n_d, body)

    def send_back_last():
        for n in range(n_dp):
            exchange(3, back, span(n, share), back_send.at[3], last_recv.at[n])

    def combine_grad_last(n, hit):
        copy = load_back(3, span(n, share), n)
        wait_landed(back.at[3, :, span(n, share)], last_recv.at[n])
        copy.start()
        copy.wait()

        def body(m):
            cols = pl.ds(pl.multiple_of(n * share + m * d_tile, d_tile), d_tile)
            tg_ref[:, cols] = (acc[1, :, cols] + dot(hit, recv[3, :, cols])).astype(BF16)
        tiles(share // d_tile, body)

    halves = (pl.ds(0, feats // 2), pl.ds(feats // 2, feats // 2))
    route(0)
    fill_tokens(0, 0)
    pl.semaphore_wait(barrier, n_exp - 1 + 2)
    send_tokens(0, halves[0])
    fill_tokens(0, 1)
    send_tokens(0, halves[1])
    fill_delta(0)
    send_delta(0)
    route(1)
    fill_tokens(1, 0)
    fill_tokens(1, 1)
    send_tokens(1, everything)
    fill_delta(1)
    send_delta(1)

    for copy in weights(0):
        copy.wait()
    tokens_landed(0)
    forward(0)
    down_part(0, lambda: turn_tokens(0), lambda: reduce_pass(0, 2))
    deltas(0)
    gate_up_part(0, 0)
    gate_up_part(0, 1)
    make_down(0, own)
    wait_sent(0, disp_send)
    outputs(0)
    send_back(0)
    wait_sent(1, disp_send)
    input_grads(0)
    send_back(1)
    for copy in weights(1):
        copy.start()

    tokens_landed(1)
    for copy in weights(1):
        copy.wait()
    forward(1)
    turn_tokens(1)
    reduce_pass(0, 0)
    wait_sent(2, disp_send)
    outputs(1)
    send_back(2)
    reduce_pass(0, 1)
    down_part(1, lambda: None, lambda: None)
    deltas(1)
    gate_up_part(1, 0)
    gate_up_part(1, 1)
    total_out(1, 1).start()
    make_down(1, own)
    wait_sent(3, disp_send)
    input_grads(1)
    send_back_last()

    for which in (2, 0, 1):
        reduce_fetch(0, which)
        reduce_end(0, which)
    combine_out(0)
    reduce_pass(1, 2)
    combine_grad_first()
    reduce_pass(1, 0)
    reduce_pass(1, 1)
    combine_out(1)
    reduce_fetch(1, 2)
    reduce_end(1, 2)
    hit = sel[1].astype(F32).T.astype(BF16)
    for n in range(n_dp - 1):
        combine_grad_last(n, hit)
    reduce_fetch(1, 0)
    reduce_end(1, 0)
    combine_grad_last(n_dp - 1, hit)
    wait_landed(land_gu.at[:, 1, 1], land_recv.at[4])

    for i in range(4):
        wait_sent(i, back_send)
    for l in range(2):
        for which in range(3):
            three = part_dn.at[l, pl.ds(0, 3)] if which == 2 else part_gu.at[l, which, pl.ds(0, 3)]
            wait_landed(three, rs_send.at[3 * l + which])
            total_out(l, which).wait()


def finish(
    lo_ref, tg_ref, gg_ref, gu_ref, land_ref, dn_ref,
    lo_out, tg_out, gg_out, gate_out, up_out, down_out,
    gu, land, dn, gate, up, down, lo, tg, gg, in_sem, out_sem, pass_sem,
):
    ins = [
        pltpu.make_async_copy(src, dst, in_sem.at[n])
        for n, (src, dst) in enumerate((
            (gu_ref.at[0, 0], gu.at[0, 0]), (gu_ref.at[0, 1], gu.at[0, 1]),
            (dn_ref.at[0], dn.at[0]), (dn_ref.at[1], dn.at[1]), (gu_ref.at[1, 0], gu.at[1, 0]),
            (gu_ref.at[1, 1], gu.at[1, 1]), (land_ref.at[0, 1, 1], land.at[0]), (land_ref.at[1, 1, 1], land.at[1]),
        ))
    ]
    for copy in ins:
        copy.start()
    rest = ((lo_ref, lo, lo_out), (tg_ref, tg, tg_out), (gg_ref, gg, gg_out))
    entering = [pltpu.make_async_copy(src, mid, pass_sem.at[0, n]) for n, (src, mid, _) in enumerate(rest)]
    through = [pltpu.make_async_copy(mid, dst, pass_sem.at[1, n]) for n, (_, mid, dst) in enumerate(rest)]
    for copy in entering:
        copy.start()
    work = (
        (ins[:1], (gu.at[0, 0],), gate.at[0], gate_out.at[0]),
        (ins[1:2], (gu.at[0, 1],), gate.at[1], gate_out.at[1]),
        (ins[2:3], (dn.at[0],), down.at[0], down_out.at[0]),
        (ins[3:4], (dn.at[1],), down.at[1], down_out.at[1]),
        (ins[4:5], (gu.at[1, 0],), up.at[0], up_out.at[0]),
        (ins[5:], (gu.at[1, 1], land.at[0], land.at[1]), up.at[1], up_out.at[1]),
    )
    outs = []
    for n, (needs, terms, made, dst) in enumerate(work):
        for copy in needs:
            copy.wait()
        step = made.shape[0] // 8

        def body(i):
            at = span(i, step)
            total = terms[0][at, :].astype(F32)
            for term in terms[1:]:
                total = total + term[at, :].astype(F32)
            made[at, :] = total

        tiles(8, body)
        outs.append(pltpu.make_async_copy(made, dst, out_sem.at[n]))
        outs[-1].start()
    for copy in entering:
        copy.wait()
    for copy in through:
        copy.start()
    for copy in through + outs:
        copy.wait()


def shards(n_dp, n_exp, tokens, expert_ids, gate_probs, w_gate, w_up, w_down, out_grad):
    tok, feats = tokens.shape
    hidden = w_gate.shape[2]
    rows = n_exp * CAP
    share = feats // n_dp
    vmem = pl.BlockSpec(memory_space=pltpu.VMEM)
    far = pl.BlockSpec(memory_space=pl.ANY)
    shape = jax.ShapeDtypeStruct
    top = expert_ids.shape[1]
    outs = pl.pallas_call(
        functools.partial(kernel, n_dp, n_exp),
        out_shape=[
            shape((tok, feats), BF16),
            shape((tok, feats), BF16),
            shape((top, tok), F32),
            shape((2, 2, share, hidden), BF16),
            shape((2, hidden, share), BF16),
            shape((2, 2, 2, share, hidden), BF16),
            shape((2, 2, hidden, share), BF16),
            shape((4, rows, feats), BF16),
        ],
        in_specs=[vmem] * 4 + [far] * 3,
        out_specs=[vmem] * 3 + [far] * 5,
        scratch_shapes=[
            pltpu.VMEM((4, rows, feats), BF16),
            pltpu.VMEM((4, rows, feats), BF16),
            pltpu.VMEM((feats, rows), BF16),
            pltpu.VMEM((feats, hidden), BF16),
            pltpu.VMEM((feats, hidden), BF16),
            pltpu.VMEM((hidden, feats), BF16),
            pltpu.VMEM((rows, hidden), BF16),
            pltpu.VMEM((hidden, rows), BF16),
            pltpu.VMEM((rows, hidden), BF16),
            pltpu.VMEM((rows, hidden), BF16),
            pltpu.VMEM((rows, hidden), F32),
            pltpu.VMEM((rows, hidden), F32),
            pltpu.VMEM((2, 2, n_dp, share, hidden), BF16),
            pltpu.VMEM((2, n_dp, hidden, share), BF16),
            pltpu.VMEM((2, 2, 2, share // 2, hidden), BF16),
            pltpu.VMEM((2, 2, hidden, share // 2), BF16),
            pltpu.VMEM((2, rows, tok), BF16),
            pltpu.VMEM((2, rows, 1), F32),
            pltpu.VMEM((2, tok, feats), F32),
            pltpu.SemaphoreType.DMA((3,)),
            pltpu.SemaphoreType.DMA((4,)),
            pltpu.SemaphoreType.DMA((2,)),
            pltpu.SemaphoreType.DMA((2, 7)),
            pltpu.SemaphoreType.DMA((4,)),
            pltpu.SemaphoreType.DMA((3,)),
            pltpu.SemaphoreType.DMA((4,)),
            pltpu.SemaphoreType.DMA((6,)),
            pltpu.SemaphoreType.DMA((6,)),
            pltpu.SemaphoreType.DMA((6,)),
            pltpu.SemaphoreType.DMA((6, 3)),
            pltpu.SemaphoreType.DMA((7,)),
        ],
        compiler_params=pltpu.CompilerParams(
            collective_id=0, has_side_effects=True, vmem_limit_bytes=62 * 2**20
        ),
        cost_estimate=pl.CostEstimate(
            flops=18 * 2 * rows * feats * hidden, bytes_accessed=60_000_000, transcendentals=4 * rows * hidden
        ),
    )(expert_ids.T, gate_probs.T, tokens, out_grad, w_gate, w_up, w_down)
    layer_out, token_grad, gate_grad, sum_gu, sum_dn, land_gu, *_ = outs
    layer_out, token_grad, gate_grad, grad_gate, grad_up, grad_down = pl.pallas_call(
        finish,
        out_shape=[
            shape((tok, feats), BF16),
            shape((tok, feats), BF16),
            shape((top, tok), F32),
            shape((2, share, hidden), F32),
            shape((2, share, hidden), F32),
            shape((2, hidden, share), F32),
        ],
        in_specs=[far] * 6,
        out_specs=[far] * 6,
        scratch_shapes=[
            pltpu.VMEM((2, 2, share, hidden), BF16),
            pltpu.VMEM((2, share, hidden), BF16),
            pltpu.VMEM((2, hidden, share), BF16),
            pltpu.VMEM((2, share, hidden), F32),
            pltpu.VMEM((2, share, hidden), F32),
            pltpu.VMEM((2, hidden, share), F32),
            pltpu.VMEM((tok, feats), BF16),
            pltpu.VMEM((tok, feats), BF16),
            pltpu.VMEM((top, tok), F32),
            pltpu.SemaphoreType.DMA((8,)),
            pltpu.SemaphoreType.DMA((6,)),
            pltpu.SemaphoreType.DMA((2, 3)),
        ],
        compiler_params=pltpu.CompilerParams(vmem_limit_bytes=62 * 2**20),
    )(layer_out, token_grad, gate_grad, sum_gu, land_gu, sum_dn)
    return layer_out, token_grad, gate_grad.T, grad_gate, grad_up, grad_down


def solution(mesh):
    tokens_at = P(("dp", "expert"), None)
    in_specs = (tokens_at,) * 3 + (P("expert", None, None),) * 3 + (tokens_at,)
    out_specs = (tokens_at,) * 3 + (
        P("expert", "dp", None),
        P("expert", "dp", None),
        P("expert", None, "dp"),
    )
    body = functools.partial(shards, mesh.shape["dp"], mesh.shape["expert"])
    return jax.shard_map(body, mesh=mesh, in_specs=in_specs, out_specs=out_specs, check_vma=False)
```

```python
import functools

import jax
import jax.numpy as jnp
from jax import lax
from jax.experimental import pallas as pl
from jax.experimental.pallas import tpu as pltpu
from jax.sharding import PartitionSpec as P

MESH = pl.DeviceIdType.MESH
F32 = jnp.float32
BF16 = jnp.bfloat16
CAP = 16
NT = (((1,), (1,)), ((), ()))
TN = (((0,), (0,)), ((), ()))


def dot(a, b, dims=(((1,), (0,)), ((), ()))):
    return lax.dot_general(a, b, dims, preferred_element_type=F32)


def tiles(count, body):
    if count == 1:
        body(0)
    else:
        lax.fori_loop(0, count, lambda i, c: (body(i), c)[1], 0)


def span(i, size):
    return pl.ds(pl.multiple_of(i * size, size), size)


def kernel(
    n_dp, n_exp,
    ids_ref, probs_ref, tok_hbm, og_hbm, wg_hbm, wu_hbm, wd_hbm,
    lo_ref, tg_ref, gg_ref, sum_gu, sum_dn, land_gu, land_dn, back,
    tok_ref, og_ref, send, recv, tt, wg, wu, wd, act, act_t, gd, ud, pre_g, pre_u,
    part_gu, part_dn, mid_gu, mid_dn, sel, pslot, acc,
    in_sem, w_sem, disp_send, tok_recv, delta_recv, back_send, back_recv, last_recv,
    rs_send, mid_recv, land_recv, sum_sem, load_sem,
):
    dp, me = lax.axis_index("dp"), lax.axis_index("expert")
    tok, feats = tok_ref.shape
    hidden = wg.shape[1]
    rows = n_exp * CAP
    top = ids_ref.shape[0]
    right, left = lax.rem(dp + 1, n_dp), lax.rem(dp + n_dp - 1, n_dp)
    across = lax.rem(dp + 2, n_dp)
    f_tile, d_tile = min(256, hidden), min(256, feats)
    n_f, n_d = hidden // f_tile, feats // d_tile
    share = feats // n_dp

    def peer(k):
        if n_exp != 32:
            return lax.rem(me + k, n_exp)
        off = lax.rem(k * 11, 32)
        z, y, c = me // 8, lax.rem(me // 2, 4), lax.rem(me, 2)
        z = lax.rem(z + off // 8, 4)
        y = lax.rem(y + lax.rem(off // 2, 4), 4)
        c = lax.rem(c + lax.rem(off, 2), 2)
        return (z * 4 + y) * 2 + c

    rows_in = [
        pltpu.make_async_copy(src, dst, in_sem.at[i])
        for i, (src, dst) in enumerate(((tok_hbm, tok_ref), (og_hbm, og_ref)))
    ]
    for copy in rows_in:
        copy.start()

    barrier = pltpu.get_barrier_semaphore()

    def greet(k, carry):
        pl.semaphore_signal(barrier, inc=1, device_id={"expert": peer(k)}, device_id_type=MESH)
        return carry

    lax.fori_loop(1, n_exp, greet, 0)
    for side in (left, right):
        pl.semaphore_signal(barrier, inc=1, device_id={"dp": side}, device_id_type=MESH)

    def weights(l):
        return [
            pltpu.make_async_copy(src.at[l], dst, w_sem.at[i])
            for i, (src, dst) in enumerate(((wg_hbm, wg), (wu_hbm, wu), (wd_hbm, wd)))
        ]

    ids_t, probs_t = ids_ref[...], probs_ref[...]
    earlier = (
        lax.broadcasted_iota(jnp.int32, (tok, tok), 0)
        < lax.broadcasted_iota(jnp.int32, (tok, tok), 1)
    ).astype(F32).astype(BF16)

    def route(l):
        expert = lax.broadcasted_iota(jnp.int32, (n_exp, tok), 0) * 2 + l
        named = jnp.zeros((n_exp, tok), F32)
        prob = jnp.zeros((n_exp, tok), F32)
        for k in range(top):
            hit = expert == ids_t[k : k + 1, :]
            named = named + jnp.where(hit, 1.0, 0.0)
            prob = prob + jnp.where(hit, probs_t[k : k + 1, :], 0.0)
        rank = dot(named.astype(BF16), earlier)
        rank = jnp.where(named > 0.0, rank, -1.0)
        slot = lax.broadcasted_iota(jnp.int32, (n_exp, CAP, tok), 1).astype(F32)
        hit = jnp.where(rank[:, None, :] == slot, 1.0, 0.0)
        weight = jnp.sum(hit * prob[:, None, :], axis=2, keepdims=True)
        hit = hit.reshape(rows, tok)
        sel[l] = hit.astype(BF16)
        pslot[l] = weight.reshape(rows, 1)

    def fill_tokens(l, h):
        def body(i):
            cols = span(i + h * (n_d // 2), d_tile)
            send[2 * l, :, cols] = dot(sel[l], tok_ref[:, cols]).astype(BF16)
        tiles(n_d // 2, body)

    def fill_delta(l):
        def body(i):
            cols = span(i, d_tile)
            send[2 * l + 1, :, cols] = (pslot[l] * dot(sel[l], og_ref[:, cols])).astype(BF16)
        tiles(n_d, body)

    def chunk(i):
        return pl.ds(pl.multiple_of(i * CAP, CAP), CAP)

    everything = pl.ds(0, feats)

    def exchange(i, land, cols, send_sem, recv_sem):
        pltpu.make_async_copy(
            send.at[i, chunk(me), cols], land.at[i, chunk(me), cols], recv_sem
        ).start()

        def body(k, carry):
            to = peer(k)
            pltpu.make_async_remote_copy(
                src_ref=send.at[i, chunk(to), cols],
                dst_ref=land.at[i, chunk(me), cols],
                send_sem=send_sem,
                recv_sem=recv_sem,
                device_id={"expert": to},
                device_id_type=MESH,
            ).start()
            return carry

        lax.fori_loop(1, n_exp, body, 0)

    def wait_sent(i, sem):
        part = send.at[i, pl.ds(0, rows - CAP)]
        pltpu.make_async_copy(part, part, sem.at[i]).wait()

    def wait_landed(view, sem):
        pltpu.make_async_copy(view, view, sem).wait()

    half_share = share // 2
    pieces = tuple(
        (j, h * half_share, half_share)
        for j, h in ((across, 0), (across, 1), (right, 1), (left, 0), (right, 0), (left, 1))
    ) + ((dp, 0, share),)
    own = len(pieces) - 1

    def piece(n):
        j, start, size = pieces[n]
        return pl.ds(pl.multiple_of(j * share + start, half_share), size)

    def send_tokens(l, cols):
        exchange(2 * l, recv, cols, disp_send.at[2 * l], tok_recv.at[l])

    def send_delta(l):
        for n in range(len(pieces)):
            exchange(2 * l + 1, recv, piece(n), disp_send.at[2 * l + 1], delta_recv.at[l, n])

    def tokens_landed(l):
        wait_landed(recv.at[2 * l], tok_recv.at[l])

    def delta_landed(l, n):
        wait_landed(recv.at[2 * l + 1, :, piece(n)], delta_recv.at[l, n])

    def send_back(i):
        exchange(i, back, everything, back_send.at[i], back_recv.at[i])

    def forward(l):
        def body(i):
            cols = span(i, f_tile)
            g = dot(recv[2 * l], wg[:, cols])
            u = dot(recv[2 * l], wu[:, cols])
            pre_g[:, cols] = g
            pre_u[:, cols] = u
            a = (g * (1.0 / (1.0 + jnp.exp(-g))) * u).astype(BF16)
            act[:, cols] = a
            act_t[cols, :] = a.T
        tiles(n_f, body)

    def turn_tokens(l):
        def body(i):
            cols = span(i, d_tile)
            tt[cols, :] = recv[2 * l, :, cols].T
        tiles(n_d, body)

    def outputs(l):
        def body(i):
            cols = span(i, d_tile)
            send[2 * l, :, cols] = dot(act[...], wd[:, cols]).astype(BF16)
        tiles(n_d, body)

    def deltas(l):
        def body(i):
            cols = span(i, f_tile)
            ad = dot(recv[2 * l + 1], wd[cols, :], NT)
            g, u = pre_g[:, cols], pre_u[:, cols]
            s = 1.0 / (1.0 + jnp.exp(-g))
            gd[:, cols] = (ad * u * s * (1.0 + g * (1.0 - s))).astype(BF16)
            ud[:, cols] = (ad * (g * s)).astype(BF16)
        tiles(n_f, body)

    def input_grads(l):
        def body(i):
            cols = span(i, d_tile)
            send[2 * l + 1, :, cols] = (
                dot(gd[...], wg[cols, :], NT) + dot(ud[...], wu[cols, :], NT)
            ).astype(BF16)
        tiles(n_d, body)

    def views(l, which):
        if which == 2:
            return part_dn.at[l], lambda s: land_dn.at[s, l], lambda s: mid_dn.at[s, l]
        return part_gu.at[l, which], lambda s: land_gu.at[s, l, which], lambda s: mid_gu.at[s, l, which]

    def post(l, which, src, dst, sem, to):
        pltpu.make_async_remote_copy(
            src_ref=src, dst_ref=dst, send_sem=rs_send.at[3 * l + which], recv_sem=sem.at[3 * l + which],
            device_id={"dp": to}, device_id_type=MESH,
        ).start()

    def half(ref, which, h):
        at = pl.ds(h * half_share, half_share)
        return ref.at[:, at] if which == 2 else ref.at[at]

    def post_across(l, which, h):
        part, _, mid = views(l, which)
        post(l, which, half(part.at[across], which, h), mid(h), mid_recv, (right, left)[h])

    def post_direct(l, which, side):
        part, land, _ = views(l, which)
        to = (right, left)[side]
        post(l, which, half(part.at[to], which, 1 - side), half(land(side), which, 1 - side), land_recv, to)

    def make_down(l, n):
        j, start, size = pieces[n]

        def body(i):
            at = span(i, f_tile)
            part_dn[l, j, at, pl.ds(start, size)] = dot(act_t[at, :], recv[2 * l + 1, :, piece(n)]).astype(BF16)

        tiles(n_f, body)

    def down_part(l, meanwhile, later):
        for h in range(2):
            delta_landed(l, h)
            make_down(l, h)
            post_across(l, 2, h)
        for side in range(2):
            delta_landed(l, 2 + side)
            make_down(l, 2 + side)
            post_direct(l, 2, side)
        meanwhile()
        for n in (4, 5):
            delta_landed(l, n)
            make_down(l, n)
        later()
        delta_landed(l, own)

    def gate_up_part(l, which):
        src = (gd, ud)[which]
        for n, j in enumerate((across, right, left, dp)):

            def body(i):
                at = span(i, d_tile)
                turned = tt[pl.ds(pl.multiple_of(j * share + i * d_tile, d_tile), d_tile), :]
                part_gu[l, which, j, at] = dot(turned, src[...]).astype(BF16)

            tiles(share // d_tile, body)
            if n == 0:
                post_across(l, which, 0)
                post_across(l, which, 1)
            elif n < 3:
                post_direct(l, which, n - 1)

    def reduce_pass(l, which):
        part, land, mid = views(l, which)
        both = mid_dn.at[:, l] if which == 2 else mid_gu.at[:, l, which]
        wait_landed(both, mid_recv.at[3 * l + which])
        for side, to in enumerate((right, left)):
            mine, passed = half(part.at[to], which, side), mid(side)

            def body(i):
                at = span(i, mine.shape[0] // 4)
                mine[at, :] = (mine[at, :].astype(F32) + passed[at, :].astype(F32)).astype(BF16)

            tiles(4, body)
            post(l, which, mine, half(land(side), which, side), land_recv, to)

    def landing(l, which, side):
        if which == 2:
            return land_dn.at[side, l], wd.at[:, pl.ds((2 * l + side) * share, share)]
        return land_gu.at[side, l, which], (wg, wu)[which].at[pl.ds((2 * l + side) * share, share)]

    def fetch(l, which):
        return [
            pltpu.make_async_copy(*landing(l, which, side), sum_sem.at[3 * l + which, side])
            for side in range(2)
        ]

    def reduce_fetch(l, which):
        both = land_dn.at[:, l] if which == 2 else land_gu.at[:, l, which]
        wait_landed(both, land_recv.at[3 * l + which])
        for copy in fetch(l, which):
            copy.start()

    def total_out(l, which):
        src, dst = (part_dn.at[l], sum_dn.at[l]) if which == 2 else (part_gu.at[l, which], sum_gu.at[which, l])
        return pltpu.make_async_copy(src.at[dp], dst, sum_sem.at[3 * l + which, 2])

    def reduce_end(l, which):
        for copy in fetch(l, which):
            copy.wait()
        part = views(l, which)[0]
        first, second = (landing(l, which, side)[1] for side in range(2))
        step = part.shape[1] // 4

        def body(i):
            at = span(i, step)
            part[dp, at] = (
                part[dp, at].astype(F32) + first[at].astype(F32) + second[at].astype(F32)
            ).astype(BF16)

        tiles(4, body)
        total_out(l, which).start()

    def load_back(i, cols, n=0):
        return pltpu.make_async_copy(back.at[i, :, cols], recv.at[i, :, cols], load_sem.at[i + n])

    def back_landed(i):
        wait_landed(back.at[i], back_recv.at[i])
        load_back(i, everything).start()

    def combine_out(l):
        i = 2 * l
        hit = sel[l].astype(F32)
        weight = (hit * pslot[l]).T
        hi = weight.astype(BF16)
        lo = (weight - hi.astype(F32)).astype(BF16)
        back_landed(i)
        load_back(i, everything).wait()

        def body(n):
            cols = span(n, d_tile)
            value = dot(hi, recv[i, :, cols]) + dot(lo, recv[i, :, cols])
            if l == 0:
                acc[0, :, cols] = value
            else:
                lo_ref[:, cols] = (acc[0, :, cols] + value).astype(BF16)
        tiles(n_d, body)
        inner = dot(recv[i], og_ref[...], NT) * hit
        inner = jnp.sum(inner.reshape(n_exp, CAP, tok), axis=1)
        expert = lax.broadcasted_iota(jnp.int32, (n_exp, tok), 0) * 2 + l
        for k in range(top):
            mine = jnp.where(expert == ids_t[k : k + 1, :], inner, 0.0)
            value = jnp.sum(mine, axis=0, keepdims=True)
            if l == 0:
                gg_ref[k : k + 1, :] = value
            else:
                gg_ref[k : k + 1, :] = gg_ref[k : k + 1, :] + value

    def combine_grad_first():
        hit = sel[0].astype(F32).T.astype(BF16)
        back_landed(1)
        load_back(1, everything).wait()

        def body(n):
            cols = span(n, d_tile)
            acc[1, :, cols] = dot(hit, recv[1, :, cols])
        tiles(n_d, body)

    def send_back_last():
        for n in range(n_dp):
            exchange(3, back, span(n, share), back_send.at[3], last_recv.at[n])

    def combine_grad_last(n, hit):
        copy = load_back(3, span(n, share), n)
        wait_landed(back.at[3, :, span(n, share)], last_recv.at[n])
        copy.start()
        copy.wait()

        def body(m):
            cols = pl.ds(pl.multiple_of(n * share + m * d_tile, d_tile), d_tile)
            tg_ref[:, cols] = (acc[1, :, cols] + dot(hit, recv[3, :, cols])).astype(BF16)
        tiles(share // d_tile, body)

    halves = (pl.ds(0, feats // 2), pl.ds(feats // 2, feats // 2))
    route(0)
    rows_in[0].wait()
    fill_tokens(0, 0)
    pl.semaphore_wait(barrier, n_exp - 1 + 2)
    send_tokens(0, halves[0])
    fill_tokens(0, 1)
    send_tokens(0, halves[1])
    rows_in[1].wait()
    for copy in weights(0):
        copy.start()
    fill_delta(0)
    send_delta(0)
    route(1)
    fill_tokens(1, 0)
    fill_tokens(1, 1)
    send_tokens(1, everything)
    fill_delta(1)
    send_delta(1)

    for copy in weights(0):
        copy.wait()
    tokens_landed(0)
    forward(0)
    down_part(0, lambda: turn_tokens(0), lambda: reduce_pass(0, 2))
    deltas(0)
    gate_up_part(0, 0)
    gate_up_part(0, 1)
    make_down(0, own)
    wait_sent(0, disp_send)
    outputs(0)
    send_back(0)
    wait_sent(1, disp_send)
    input_grads(0)
    send_back(1)
    for copy in weights(1):
        copy.start()

    tokens_landed(1)
    for copy in weights(1):
        copy.wait()
    forward(1)
    turn_tokens(1)
    reduce_pass(0, 0)
    wait_sent(2, disp_send)
    outputs(1)
    send_back(2)
    reduce_pass(0, 1)
    down_part(1, lambda: None, lambda: None)
    deltas(1)
    gate_up_part(1, 0)
    gate_up_part(1, 1)
    total_out(1, 1).start()
    make_down(1, own)
    wait_sent(3, disp_send)
    input_grads(1)
    send_back_last()

    for which in (2, 0, 1):
        reduce_fetch(0, which)
        reduce_end(0, which)
    combine_out(0)
    reduce_pass(1, 2)
    combine_grad_first()
    reduce_pass(1, 0)
    reduce_pass(1, 1)
    combine_out(1)
    reduce_fetch(1, 2)
    reduce_end(1, 2)
    hit = sel[1].astype(F32).T.astype(BF16)
    for n in range(n_dp - 1):
        combine_grad_last(n, hit)
    reduce_fetch(1, 0)
    reduce_end(1, 0)
    combine_grad_last(n_dp - 1, hit)
    wait_landed(land_gu.at[:, 1, 1], land_recv.at[4])

    for i in range(4):
        wait_sent(i, back_send)
    for l in range(2):
        for which in range(3):
            three = part_dn.at[l, pl.ds(0, 3)] if which == 2 else part_gu.at[l, which, pl.ds(0, 3)]
            wait_landed(three, rs_send.at[3 * l + which])
            total_out(l, which).wait()


def finish(
    lo_ref, tg_ref, gg_ref, gu_ref, land_ref, dn_ref,
    lo_out, tg_out, gg_out, gate_out, up_out, down_out,
    gu, land, dn, gate, up, down, lo, tg, gg, in_sem, out_sem, pass_sem,
):
    ins = [
        pltpu.make_async_copy(src, dst, in_sem.at[n])
        for n, (src, dst) in enumerate((
            (gu_ref.at[0, 0], gu.at[0, 0]), (gu_ref.at[0, 1], gu.at[0, 1]),
            (dn_ref.at[0], dn.at[0]), (dn_ref.at[1], dn.at[1]), (gu_ref.at[1, 0], gu.at[1, 0]),
            (gu_ref.at[1, 1], gu.at[1, 1]), (land_ref.at[0, 1, 1], land.at[0]), (land_ref.at[1, 1, 1], land.at[1]),
        ))
    ]
    for copy in ins:
        copy.start()
    rest = ((lo_ref, lo, lo_out), (tg_ref, tg, tg_out), (gg_ref, gg, gg_out))
    entering = [pltpu.make_async_copy(src, mid, pass_sem.at[0, n]) for n, (src, mid, _) in enumerate(rest)]
    through = [pltpu.make_async_copy(mid, dst, pass_sem.at[1, n]) for n, (_, mid, dst) in enumerate(rest)]
    for copy in entering:
        copy.start()
    work = (
        (ins[:1], (gu.at[0, 0],), gate.at[0], gate_out.at[0]),
        (ins[1:2], (gu.at[0, 1],), gate.at[1], gate_out.at[1]),
        (ins[2:3], (dn.at[0],), down.at[0], down_out.at[0]),
        (ins[3:4], (dn.at[1],), down.at[1], down_out.at[1]),
        (ins[4:5], (gu.at[1, 0],), up.at[0], up_out.at[0]),
        (ins[5:], (gu.at[1, 1], land.at[0], land.at[1]), up.at[1], up_out.at[1]),
    )
    outs = []
    for n, (needs, terms, made, dst) in enumerate(work):
        for copy in needs:
            copy.wait()
        step = made.shape[0] // 8

        def body(i):
            at = span(i, step)
            total = terms[0][at, :].astype(F32)
            for term in terms[1:]:
                total = total + term[at, :].astype(F32)
            made[at, :] = total

        tiles(8, body)
        outs.append(pltpu.make_async_copy(made, dst, out_sem.at[n]))
        outs[-1].start()
    for copy in entering:
        copy.wait()
    for copy in through:
        copy.start()
    for copy in through + outs:
        copy.wait()


def shards(n_dp, n_exp, tokens, expert_ids, gate_probs, w_gate, w_up, w_down, out_grad):
    tok, feats = tokens.shape
    hidden = w_gate.shape[2]
    rows = n_exp * CAP
    share = feats // n_dp
    vmem = pl.BlockSpec(memory_space=pltpu.VMEM)
    far = pl.BlockSpec(memory_space=pl.ANY)
    shape = jax.ShapeDtypeStruct
    top = expert_ids.shape[1]
    outs = pl.pallas_call(
        functools.partial(kernel, n_dp, n_exp),
        out_shape=[
            shape((tok, feats), BF16),
            shape((tok, feats), BF16),
            shape((top, tok), F32),
            shape((2, 2, share, hidden), BF16),
            shape((2, hidden, share), BF16),
            shape((2, 2, 2, share, hidden), BF16),
            shape((2, 2, hidden, share), BF16),
            shape((4, rows, feats), BF16),
        ],
        in_specs=[vmem] * 2 + [far] * 5,
        out_specs=[vmem] * 3 + [far] * 5,
        scratch_shapes=[
            pltpu.VMEM((tok, feats), BF16),
            pltpu.VMEM((tok, feats), BF16),
            pltpu.VMEM((4, rows, feats), BF16),
            pltpu.VMEM((4, rows, feats), BF16),
            pltpu.VMEM((feats, rows), BF16),
            pltpu.VMEM((feats, hidden), BF16),
            pltpu.VMEM((feats, hidden), BF16),
            pltpu.VMEM((hidden, feats), BF16),
            pltpu.VMEM((rows, hidden), BF16),
            pltpu.VMEM((hidden, rows), BF16),
            pltpu.VMEM((rows, hidden), BF16),
            pltpu.VMEM((rows, hidden), BF16),
            pltpu.VMEM((rows, hidden), F32),
            pltpu.VMEM((rows, hidden), F32),
            pltpu.VMEM((2, 2, n_dp, share, hidden), BF16),
            pltpu.VMEM((2, n_dp, hidden, share), BF16),
            pltpu.VMEM((2, 2, 2, share // 2, hidden), BF16),
            pltpu.VMEM((2, 2, hidden, share // 2), BF16),
            pltpu.VMEM((2, rows, tok), BF16),
            pltpu.VMEM((2, rows, 1), F32),
            pltpu.VMEM((2, tok, feats), F32),
            pltpu.SemaphoreType.DMA((2,)),
            pltpu.SemaphoreType.DMA((3,)),
            pltpu.SemaphoreType.DMA((4,)),
            pltpu.SemaphoreType.DMA((2,)),
            pltpu.SemaphoreType.DMA((2, 7)),
            pltpu.SemaphoreType.DMA((4,)),
            pltpu.SemaphoreType.DMA((3,)),
            pltpu.SemaphoreType.DMA((4,)),
            pltpu.SemaphoreType.DMA((6,)),
            pltpu.SemaphoreType.DMA((6,)),
            pltpu.SemaphoreType.DMA((6,)),
            pltpu.SemaphoreType.DMA((6, 3)),
            pltpu.SemaphoreType.DMA((7,)),
        ],
        compiler_params=pltpu.CompilerParams(
            collective_id=0, has_side_effects=True, vmem_limit_bytes=62 * 2**20
        ),
        cost_estimate=pl.CostEstimate(
            flops=18 * 2 * rows * feats * hidden, bytes_accessed=60_000_000, transcendentals=4 * rows * hidden
        ),
    )(expert_ids.T, gate_probs.T, tokens, out_grad, w_gate, w_up, w_down)
    layer_out, token_grad, gate_grad, sum_gu, sum_dn, land_gu, *_ = outs
    layer_out, token_grad, gate_grad, grad_gate, grad_up, grad_down = pl.pallas_call(
        finish,
        out_shape=[
            shape((tok, feats), BF16),
            shape((tok, feats), BF16),
            shape((top, tok), F32),
            shape((2, share, hidden), F32),
            shape((2, share, hidden), F32),
            shape((2, hidden, share), F32),
        ],
        in_specs=[far] * 6,
        out_specs=[far] * 6,
        scratch_shapes=[
            pltpu.VMEM((2, 2, share, hidden), BF16),
            pltpu.VMEM((2, share, hidden), BF16),
            pltpu.VMEM((2, hidden, share), BF16),
            pltpu.VMEM((2, share, hidden), F32),
            pltpu.VMEM((2, share, hidden), F32),
            pltpu.VMEM((2, hidden, share), F32),
            pltpu.VMEM((tok, feats), BF16),
            pltpu.VMEM((tok, feats), BF16),
            pltpu.VMEM((top, tok), F32),
            pltpu.SemaphoreType.DMA((8,)),
            pltpu.SemaphoreType.DMA((6,)),
            pltpu.SemaphoreType.DMA((2, 3)),
        ],
        compiler_params=pltpu.CompilerParams(vmem_limit_bytes=62 * 2**20),
    )(layer_out, token_grad, gate_grad, sum_gu, land_gu, sum_dn)
    return layer_out, token_grad, gate_grad.T, grad_gate, grad_up, grad_down


def solution(mesh):
    tokens_at = P(("dp", "expert"), None)
    in_specs = (tokens_at,) * 3 + (P("expert", None, None),) * 3 + (tokens_at,)
    out_specs = (tokens_at,) * 3 + (
        P("expert", "dp", None),
        P("expert", "dp", None),
        P("expert", None, "dp"),
    )
    body = functools.partial(shards, mesh.shape["dp"], mesh.shape["expert"])
    return jax.shard_map(body, mesh=mesh, in_specs=in_specs, out_specs=out_specs, check_vma=False)
```
